128 devices in a mesh: item: 8 (over z, core), list: 16 (over y, x).
Axes of the slice: x: 4, y: 4, z: 4, core: 2. Of those that a mesh axis runs over, the one named last changes fastest.
Arguments:
- items: bfloat16 [32768, 256], P('item', 'list'), may hold values from -6 to 6
- item_weight: float32 [32768], P('item'), may hold values from 1 to 10
- list_capacity: float32 [32768], P('list'), may hold values from 1 to 10
- centroids: bfloat16 [32768, 256], P('list'), may hold values from -6 to 6
Outputs:
- new_centroids: bfloat16 [32768, 256], P('list')
The draws below stay inside these ranges and needn't reach their ends.
All inputs are finite; a program needn't handle non-finite values.
Results may differ from the reference program's by a relative error of at most 0.015.
Values may be sent and summed in bfloat16 or wider, within the bound.
No kernel may reach another device: no remote copies, remote signals or barrier semaphores. Data moves between devices by JAX's collectives and lax.ppermute only.
A program may use at most 128 MiB of HBM per device.

```python
import math
import jax
import jax.numpy as jnp
from jax import lax

E = 256
ITEM_DEV = 4096
ITERS = 3
ITEMS = 32768
LISTS = 32768
N_ITEM = 8


cluster_count = 32


def cluster_parts(key):
    centers = jax.random.normal(key, (cluster_count, E), jnp.float32)
    return centers


def draw_items(key, part):
    centers = cluster_parts(key)
    key = jax.random.fold_in(key, 3)
    key_one, key_two, key_three = jax.random.split(key, 3)
    chosen = jnp.minimum(jax.random.randint(key_one, (ITEMS,), 0, cluster_count), jax.random.randint(key_two, (ITEMS,), 0, cluster_count))
    jitter = jax.random.normal(key_three, (ITEMS, E), jnp.float32)
    values = 0.5 * centers[chosen] + jitter
    return jnp.clip(values, -6.0, 6.0).astype(jnp.bfloat16)


def draw_centroids(key, part):
    centers = cluster_parts(key)
    key = jax.random.fold_in(key, 5)
    key_one, key_two = jax.random.split(key, 2)
    chosen = jax.random.randint(key_one, (LISTS,), 0, cluster_count)
    jitter = jax.random.normal(key_two, (LISTS, E), jnp.float32)
    values = 0.5 * centers[chosen] + jitter
    return jnp.clip(values, -6.0, 6.0).astype(jnp.bfloat16)


def block_scale(key, extent, shards, least, top_value):
    loudness = 1.0
    for position, shards_of in shards:
        steps = jax.random.uniform(jax.random.fold_in(jax.random.fold_in(key, 6), position), (shards_of,), jnp.float32, least / len(shards), top_value / len(shards))
        loudness = loudness * jnp.repeat(jnp.exp(steps), extent[position] // shards_of).reshape((-1,) + (1,) * (len(extent) - 1 - position))
    return loudness


def setup_inputs(seed: int = 0) -> dict:
    key_list = jax.random.split(jax.random.key(seed), 5)
    return {
        "items": draw_items(jax.random.fold_in(key_list[4], 71), 0),
        "item_weight": jnp.clip(jnp.exp(math.log(10.0) - 2.3025851 * jax.random.uniform(key_list[1], (ITEMS,), jnp.float32) ** block_scale(key_list[1], (ITEMS,), ((0, 8),), -0.2, 0.2)), 1.0, 10.0),
        "list_capacity": jnp.clip(jnp.exp(math.log(10.0) - 2.3025851 * jax.random.uniform(key_list[2], (LISTS,), jnp.float32) ** block_scale(key_list[2], (LISTS,), ((0, 16),), -0.2, 0.2)), 1.0, 10.0),
        "centroids": draw_centroids(jax.random.fold_in(key_list[4], 71), 0),
    }


epsilon = 1e-06

def unit_rows(values):
    values = values.astype(jnp.float32)
    square = lax.optimization_barrier(jnp.mean(values * values, axis=-1, keepdims=True))
    return values * lax.rsqrt(square + epsilon) * values.shape[-1] ** (-0.5)

def reference(items, item_weight, list_capacity, centroids):
    sharpness = 2.5 * math.sqrt(E)
    item_unit = unit_rows(items).astype(jnp.bfloat16)
    list_unit = unit_rows(centroids).astype(jnp.bfloat16)
    blocks = item_unit.reshape(N_ITEM, ITEM_DEV, E)
    weights = item_weight.reshape(N_ITEM, ITEM_DEV)

    def kernel(block):
        return jnp.exp(sharpness * jnp.dot(block, list_unit.T, preferred_element_type=jnp.float32))
    col_scale = jnp.ones((LISTS,), jnp.float32)
    row_scale = None
    for step in range(ITERS):

        def sweep(total, pair):
            block, weight = pair
            tile = kernel(block)
            scale = weight / jnp.dot(tile, col_scale, precision=lax.Precision.HIGHEST)
            return (total + jnp.dot(scale, tile, precision=lax.Precision.HIGHEST), scale)
        column, row_scale = lax.scan(sweep, jnp.zeros((LISTS,), jnp.float32), (blocks, weights))
        col_scale = list_capacity / column

    def gather_sums(total, pair):
        block, scale = pair
        plan = (scale[:, None] * kernel(block) * col_scale[None, :]).astype(jnp.bfloat16)
        term = lax.dot_general(plan, block, (((0,), (0,)), ((), ())), preferred_element_type=jnp.float32)
        rounded = lax.optimization_barrier(term.astype(jnp.bfloat16))
        return (total + rounded.astype(jnp.float32), None)
    totals, unused = lax.scan(gather_sums, jnp.zeros((LISTS, E), jnp.float32), (blocks, row_scale))
    mixed = 0.1 * list_unit.astype(jnp.float32) + totals / list_capacity[:, None]
    return unit_rows(mixed).astype(jnp.bfloat16)
```

```python
import functools
import math

import jax
import jax.numpy as jnp
from jax import lax
from jax.experimental import pallas as pl
from jax.experimental.pallas import tpu as pltpu
from jax.sharding import PartitionSpec as P

E = 256
ITERS = 3
EPS = 1e-06
SHARP = 2.5 * math.sqrt(E) * math.log2(math.e)

ITEM_DEV = 4096
LIST_DEV = 2048
N_ITEM = 8
N_LIST = 16

F32 = jnp.float32
BF16 = jnp.bfloat16
VMEM = pltpu.VMEM
PARAMS = pltpu.CompilerParams(vmem_limit_bytes=12 << 20)


def whole():
    return pl.BlockSpec(memory_space=VMEM)


def in_vmem(x):
    return pltpu.with_memory_space_constraint(x, VMEM)


def unit(values, axis):
    square = jnp.mean(values * values, axis=axis, keepdims=True)
    return values * lax.rsqrt(square + EPS) * E ** (-0.5)


def put_rows(total, out_ref):
    for k in range(16):
        row = total[:, 256 * k : 256 * (k + 1)].astype(BF16)
        out_ref[:, k : k + 1, :] = jnp.broadcast_to(row[None], (N_LIST, 1, 256))


def gen_body(feat_ref, cent_ref, kern_ref, item_ref, list_ref, rows_ref, total_ref):
    @pl.loop(0, LIST_DEV // 256)
    def _(m):
        at = pl.ds(pl.multiple_of(m * 256, 256), 256)
        list_ref[at, :] = unit(cent_ref[at, :].astype(F32), 1).astype(BF16)

    @pl.loop(0, ITEM_DEV // 256)
    def _(n):
        at = pl.ds(pl.multiple_of(n * 256, 256), 256)
        block = unit(feat_ref[:, at].astype(F32), 0).astype(BF16)
        item_ref[:, at] = block
        total = jnp.zeros((8, 256), F32)
        for m in range(LIST_DEV // 256):
            rows = slice(256 * m, 256 * (m + 1))
            score = jnp.dot(list_ref[rows, :], block, preferred_element_type=F32)
            value = jnp.exp2(score * SHARP)
            kern_ref[rows, at] = value
            total = total + value.reshape(32, 8, 256).sum(0)
        total_ref[:, at] = total.sum(0, keepdims=True)

    put_rows(total_ref[...], rows_ref)


def gen(feat, cent):
    return pl.pallas_call(
        gen_body,
        out_shape=(
            VMEM((LIST_DEV, ITEM_DEV), F32),
            VMEM((E, ITEM_DEV), BF16),
            VMEM((LIST_DEV, E), BF16),
            VMEM((N_LIST, 16, 256), BF16),
        ),
        in_specs=[whole()] * 2,
        out_specs=(whole(),) * 4,
        scratch_shapes=[VMEM((1, ITEM_DEV), F32)],
        cost_estimate=pl.CostEstimate(flops=2 * LIST_DEV * ITEM_DEV * E, bytes_accessed=1 << 22, transcendentals=LIST_DEV * ITEM_DEV),
        compiler_params=PARAMS,
        name="generate",
    )(feat, cent)


def spread_rows(parts_ref, weight_ref, scale_ref):
    total = parts_ref[...].astype(F32).sum(0)
    scale = weight_ref[...] / total
    for k in range(16):
        scale_ref[:, 256 * k : 256 * (k + 1)] = jnp.broadcast_to(scale[k : k + 1, :], (8, 256))


def lanes_of(partial):
    m = partial.shape[0] // 128
    return jnp.concatenate([partial[128 * k : 128 * (k + 1)].T.sum(0, keepdims=True) for k in range(m)], 0)


def col_sums(kern_ref, scale_ref, partial_ref):
    @pl.loop(0, LIST_DEV // 64)
    def _(m):
        at = pl.ds(pl.multiple_of(m * 64, 64), 64)
        total = jnp.zeros((8, 8, 128), F32)
        for n in range(ITEM_DEV // 128):
            lanes = slice(128 * n, 128 * (n + 1))
            total = total + kern_ref[at, lanes].reshape(8, 8, 128) * scale_ref[:, lanes][None]
        partial_ref[at, :] = total.reshape(64, 128)


def col_body(kern_ref, parts_ref, weight_ref, out_ref, scale_ref, partial_ref):
    spread_rows(parts_ref, weight_ref, scale_ref)
    col_sums(kern_ref, scale_ref, partial_ref)
    out_ref[...] = lanes_of(partial_ref[...])


def col_pass(kern, parts, weight):
    return pl.pallas_call(
        col_body,
        out_shape=VMEM((16, 128), F32),
        in_specs=[whole()] * 3,
        out_specs=whole(),
        scratch_shapes=[VMEM((8, ITEM_DEV), F32), VMEM((LIST_DEV, 128), F32)],
        cost_estimate=pl.CostEstimate(flops=2 * LIST_DEV * ITEM_DEV, bytes_accessed=1 << 22, transcendentals=0),
        compiler_params=PARAMS,
        name="columns",
    )(in_vmem(kern), parts, weight)


def row_body(kern_ref, cols_ref, cap_ref, out_ref, scale_ref, total_ref):
    scale = cap_ref[...] / cols_ref[...]
    for k in range(16):
        scale_ref[128 * k : 128 * (k + 1), :] = jnp.broadcast_to(scale[k : k + 1, :], (128, 128)).T

    @pl.loop(0, ITEM_DEV // 1024)
    def _(n):
        first = pl.multiple_of(n * 1024, 1024)
        total = tuple(jnp.zeros((8, 128), F32) for _ in range(8))

        def step(m, total):
            at = pl.ds(pl.multiple_of(m * 64, 64), 64)
            by = scale_ref[at, :].reshape(8, 8, 128)
            block = kern_ref[at, pl.ds(first, 1024)].reshape(8, 8, 1024)
            total = list(total)
            for j in range(8):
                for k in range(8):
                    total[k] = total[k] + block[j, :, 128 * k : 128 * (k + 1)] * by[j]
            return tuple(total)

        total = lax.fori_loop(0, LIST_DEV // 64, step, total)
        for k in range(8):
            total_ref[:, pl.ds(pl.multiple_of(first + 128 * k, 128), 128)] = total[k].sum(0, keepdims=True)

    put_rows(total_ref[...], out_ref)


def row_pass(kern, cols, cap):
    return pl.pallas_call(
        row_body,
        out_shape=VMEM((N_LIST, 16, 256), BF16),
        in_specs=[whole()] * 3,
        out_specs=whole(),
        scratch_shapes=[VMEM((LIST_DEV, 128), F32), VMEM((1, ITEM_DEV), F32)],
        cost_estimate=pl.CostEstimate(flops=2 * LIST_DEV * ITEM_DEV, bytes_accessed=1 << 22, transcendentals=0),
        compiler_params=PARAMS,
        name="rows",
    )(in_vmem(kern), cols, cap)


def last_body(kern_ref, item_ref, parts_ref, weight_ref, out_ref, cols_ref, scale_ref, mixed_ref):
    spread_rows(parts_ref, weight_ref, scale_ref)

    @pl.loop(0, ITEM_DEV // 256)
    def _(n):
        at = pl.ds(pl.multiple_of(n * 256, 256), 256)
        mixed_ref[at, :] = (item_ref[:, at].astype(F32) * scale_ref[:1, at]).T.astype(BF16)

    for b in range(LIST_DEV // 128):
        rows = slice(128 * b, 128 * (b + 1))
        block = kern_ref[rows, :]
        out_ref[rows, :] = jnp.dot(block.astype(BF16), mixed_ref[...], preferred_element_type=F32).astype(BF16)
        total = jnp.zeros((16, 8, 128), F32)
        for n in range(ITEM_DEV // 128):
            lanes = slice(128 * n, 128 * (n + 1))
            total = total + kern_ref[rows, lanes].reshape(16, 8, 128) * scale_ref[:, lanes][None]
        cols_ref[b : b + 1, :] = total.reshape(128, 128).T.sum(0, keepdims=True)


def last_pass(kern, item, parts, weight):
    return pl.pallas_call(
        last_body,
        out_shape=(VMEM((LIST_DEV, E), BF16), VMEM((16, 128), F32)),
        in_specs=[whole()] * 4,
        out_specs=(whole(),) * 2,
        scratch_shapes=[VMEM((8, ITEM_DEV), F32), VMEM((ITEM_DEV, E), BF16)],
        cost_estimate=pl.CostEstimate(flops=2 * LIST_DEV * ITEM_DEV * E, bytes_accessed=1 << 22, transcendentals=0),
        compiler_params=PARAMS,
        name="totals",
    )(in_vmem(kern), item, parts, weight)


def swap_core(x):
    return lax.ppermute(x, "item", [(i, i ^ 1) for i in range(N_ITEM)])


def along_z(x, step):
    return lax.ppermute(x, "item", [(i, (i + 2 * step) % N_ITEM) for i in range(N_ITEM)])


def sum_cols(x):
    x = x + swap_core(x)
    return x + along_z(x, 1) + along_z(x, 3) + along_z(x, 2)


def share_rows(parts):
    return lax.all_to_all(parts, "list", 0, 0)


def local(items, item_weight, list_capacity, centroids):
    core = lax.axis_index("item") % 2
    z = lax.axis_index("item") // 2
    feat = items.T
    feat = lax.all_to_all(jnp.broadcast_to(feat[None], (N_LIST,) + feat.shape), "list", 0, 0)
    feat = feat.reshape(E, ITEM_DEV)
    weight = item_weight.reshape(16, 256)
    cap = list_capacity.reshape(16, 128)

    kern, item, lists, parts = gen(feat, centroids)
    for step in range(ITERS - 1):
        cols = sum_cols(col_pass(kern, share_rows(parts), weight))
        parts = row_pass(kern, cols, cap)
    mixed, cols = last_pass(kern, item, share_rows(parts), weight)

    mixed = mixed.reshape(2, 4, 256, E)
    cols = cols.reshape(2, 4, 256)
    half = lax.dynamic_index_in_dim(mixed, core, 0, False).astype(F32)
    half = half + swap_core(lax.dynamic_index_in_dim(mixed, 1 - core, 0, False)).astype(F32)
    tops = lax.dynamic_index_in_dim(cols, core, 0, False) + swap_core(lax.dynamic_index_in_dim(cols, 1 - core, 0, False))
    high = tops.astype(BF16)
    low = (tops - high.astype(F32)).astype(BF16)
    pad = jnp.zeros((4, 14, E), BF16)
    sent = jnp.concatenate([half.astype(BF16), high[:, None], low[:, None], pad], 1)

    def piece(d):
        return lax.dynamic_index_in_dim(sent, (z + d) % 4, 0, False)

    mine = [piece(0)] + [along_z(piece(d), d) for d in (1, 3, 2)]
    mine = sum(m.astype(F32) for m in mine)
    totals, col_total = mine[:256], mine[256] + mine[257]
    first = core * 1024 + z * 256
    own = lax.dynamic_slice_in_dim(lists, first, 256, 0)
    done = unit(0.1 * own.astype(F32) + totals / col_total[:, None], 1).astype(BF16)

    out = jnp.zeros((4, 256, E), BF16)
    out = lax.dynamic_update_index_in_dim(out, done, z, 0)
    for d in (1, 3, 2):
        out = lax.dynamic_update_index_in_dim(out, along_z(done, d), (z - d) % 4, 0)
    other = swap_core(out)
    both = jnp.zeros((2, 4, 256, E), BF16)
    both = lax.dynamic_update_index_in_dim(both, out, core, 0)
    both = lax.dynamic_update_index_in_dim(both, other, 1 - core, 0)
    return both.reshape(LIST_DEV, E)


def solution(mesh):
    placed = (P("item", "list"), P("item"), P("list"), P("list", None))
    return jax.shard_map(
        local, mesh=mesh, in_specs=placed, out_specs=P("list", None), check_vma=False
    )
```

```python
import functools
import math

import jax
import jax.numpy as jnp
from jax import lax
from jax.experimental import pallas as pl
from jax.experimental.pallas import tpu as pltpu
from jax.sharding import PartitionSpec as P

E = 256
ITERS = 3
EPS = 1e-06
SHARP = 2.5 * math.sqrt(E) * math.log2(math.e)

ITEM_DEV = 4096
LIST_DEV = 2048
HALF = ITEM_DEV // 2
QUART = ITEM_DEV // 4
N_ITEM = 8
N_LIST = 16

F32 = jnp.float32
BF16 = jnp.bfloat16
VMEM = pltpu.VMEM


def whole(n):
    return [pl.BlockSpec(memory_space=VMEM)] * n


def call(body, args, out, scratch, name, flops=0, limit=4):
    return pl.pallas_call(
        body,
        out_shape=out,
        in_specs=whole(len(args)),
        out_specs=tuple(whole(len(out))) if isinstance(out, tuple) else whole(1)[0],
        scratch_shapes=scratch,
        compiler_params=pltpu.CompilerParams(vmem_limit_bytes=limit << 20),
        cost_estimate=pl.CostEstimate(flops=flops, bytes_accessed=1 << 20, transcendentals=0),
        name=name,
    )(*args)


def unit(values, axis):
    square = jnp.mean(values * values, axis=axis, keepdims=True)
    return values * lax.rsqrt(square + EPS) * E ** (-0.5)


def place():
    item = lax.axis_index("item")
    spot = lax.axis_index("list")
    return item % 2, item // 2, spot // 4, spot % 4


def shift(name, step):
    def along(i):
        if name == "x":
            return i // 4 * 4 + (i + step) % 4
        if name == "y":
            return (i + 4 * step) % N_LIST
        return (i + 2 * step) % N_ITEM

    axis, size = ("item", N_ITEM) if name == "z" else ("list", N_LIST)
    return lambda block: lax.ppermute(block, axis, [(i, along(i)) for i in range(size)])


def swap_core(block):
    return lax.ppermute(block, "item", [(i, i ^ 1) for i in range(N_ITEM)])


ORDER = (0, -1, 1, 2)


def gather_small(block, axis):
    return [block, shift(axis, 1)(block), shift(axis, 3)(block), shift(axis, 2)(block)]


def gather_large(block, axis):
    left, right = shift(axis, 1)(block), shift(axis, 3)(block)
    n = block.shape[0] // 2
    return [block, left, right, shift(axis, 1)(left[:n]), shift(axis, 3)(right[n:])]


def prep_body(cent_ref, weight_ref, cap_ref, list_ref, weight_out_ref, cap_out_ref):
    weight_out_ref[...] = weight_ref[...]
    cap_out_ref[...] = cap_ref[...]
    for m in range(LIST_DEV // 256):
        at = slice(256 * m, 256 * (m + 1))
        list_ref[at, :] = unit(cent_ref[at, :].astype(F32), 1).astype(BF16)


def prep(cent, weight, cap):
    out = (VMEM((LIST_DEV, E), BF16), VMEM((16, 256), F32), VMEM((16, 128), F32))
    return call(prep_body, (cent, weight, cap), out, [], "lists")


def put_rows(total, out_ref):
    for k in range(16):
        row = total[:, 256 * k : 256 * (k + 1)].astype(BF16)
        out_ref[:, k : k + 1, :] = jnp.broadcast_to(row[None], (N_LIST, 1, 256))


TILE_M = 512


def gen_body(last, list_ref, own_ref, left_ref, right_ref, low_ref, high_ref, *refs):
    if last:
        before_ref, *kern_refs, item_ref, rows_ref, feat_ref, total_ref = refs
    else:
        *kern_refs, item_ref, total_ref, feat_ref = refs
    _, _, y, x = place()
    for i, outer in enumerate(ORDER):
        for j, inner in enumerate(ORDER):
            if i < 3:
                block = (own_ref, left_ref, right_ref)[i][16 * j : 16 * (j + 1), :]
            else:
                block = (low_ref, high_ref)[j // 2][16 * (j % 2) : 16 * (j % 2 + 1), :]
            if last:
                spot = (y + inner + 4) % 4 * 4 + (x + outer + 4) % 4
            else:
                spot = (y + outer + 4) % 4 * 4 + (x + inner + 4) % 4
            feat_ref[pl.ds(pl.multiple_of(spot * 16, 16), 16), :] = block

    for n, kern_ref in enumerate(kern_refs):
        at = slice(QUART * n, QUART * (n + 1))
        block = unit(feat_ref[:, at].astype(F32), 0)
        item_ref[at, :] = block.T.astype(BF16)
        block = block.astype(BF16)

        def step(m, total):
            rows = pl.ds(pl.multiple_of(m * TILE_M, TILE_M), TILE_M)
            score = jnp.dot(list_ref[rows, :], block, preferred_element_type=F32)
            value = jnp.exp2(score * SHARP)
            kern_ref[rows, :] = value
            return total + value.reshape(TILE_M // 8, 8, QUART).sum(0)

        total = lax.fori_loop(0, LIST_DEV // TILE_M, step, jnp.zeros((8, QUART), F32))
        total_ref[:, at] = total.sum(0, keepdims=True)

    if last:
        put_rows(jnp.concatenate([before_ref[...], total_ref[...]], 1), rows_ref)


def gen(last, lists, pieces, before=()):
    out = (VMEM((LIST_DEV, QUART), F32),) * 2 + (VMEM((HALF, E), BF16),)
    scratch = [VMEM((E, HALF), BF16)]
    if last:
        out += (VMEM((N_LIST, 16, 256), BF16),)
        scratch += [VMEM((1, HALF), F32)]
    else:
        out += (VMEM((1, HALF), F32),)
    return call(
        functools.partial(gen_body, last), (lists, *pieces, *before), out, scratch, "generate",
        2 * LIST_DEV * HALF * E, 8,
    )


def spread_rows(parts_ref, weight_ref, scale_ref):
    scale = weight_ref[...] / parts_ref[...].astype(F32).sum(0)
    for k in range(16):
        scale_ref[:, 256 * k : 256 * (k + 1)] = jnp.broadcast_to(scale[k : k + 1, :], (8, 256))


def lanes_of(partial):
    m = partial.shape[0] // 128
    return jnp.concatenate([partial[128 * k : 128 * (k + 1)].T.sum(0, keepdims=True) for k in range(m)], 0)


def col_body(*refs):
    *kern_refs, parts_ref, weight_ref, out_ref, scale_ref, partial_ref = refs
    spread_rows(parts_ref, weight_ref, scale_ref)

    @pl.loop(0, LIST_DEV // 64)
    def _(m):
        at = pl.ds(pl.multiple_of(m * 64, 64), 64)
        total = jnp.zeros((8, 8, 128), F32)
        for h, ref in enumerate(kern_refs):
            for n in range(QUART // 128):
                by = scale_ref[:, QUART * h + 128 * n : QUART * h + 128 * (n + 1)]
                total = total + ref[at, 128 * n : 128 * (n + 1)].reshape(8, 8, 128) * by[None]
        partial_ref[at, :] = total.reshape(64, 128)

    out_ref[...] = jnp.broadcast_to(lanes_of(partial_ref[...])[None], (N_ITEM, 16, 128))


def col_pass(kern, parts, weight):
    return call(
        col_body, (*kern, parts, weight), VMEM((N_ITEM, 16, 128), F32),
        [VMEM((8, ITEM_DEV), F32), VMEM((LIST_DEV, 128), F32)], "columns", 2 * LIST_DEV * ITEM_DEV,
    )


def row_body(*refs):
    *kern_refs, cols_ref, cap_ref, out_ref, scale_ref, total_ref = refs
    scale = cap_ref[...] / cols_ref[...].sum(0)
    for k in range(16):
        scale_ref[128 * k : 128 * (k + 1), :] = jnp.broadcast_to(scale[k : k + 1, :], (128, 128)).T

    for h, ref in enumerate(kern_refs):

        def step(m, total):
            at = pl.ds(pl.multiple_of(m * 64, 64), 64)
            by = scale_ref[at, :].reshape(8, 8, 128)
            block = ref[at, :].reshape(8, 8, QUART)
            total = list(total)
            for j in range(8):
                for k in range(8):
                    total[k] = total[k] + block[j, :, 128 * k : 128 * (k + 1)] * by[j]
            return tuple(total)

        total = lax.fori_loop(0, LIST_DEV // 64, step, (jnp.zeros((8, 128), F32),) * 8)
        for k in range(8):
            first = QUART * h + 128 * k
            total_ref[:, first : first + 128] = total[k].sum(0, keepdims=True)

    put_rows(total_ref[...], out_ref)


def row_pass(kern, cols, cap):
    return call(
        row_body, (*kern, cols, cap), VMEM((N_LIST, 16, 256), BF16),
        [VMEM((LIST_DEV, 128), F32), VMEM((1, ITEM_DEV), F32)], "rows", 2 * LIST_DEV * ITEM_DEV,
    )


TILE_L = 256


def last_body(other, *refs):
    *kern_refs, item_one_ref, item_two_ref, parts_ref, weight_ref, out_ref, scale_ref, partial_ref = refs
    core, _, _, _ = place()
    base = (1 - core if other else core) * 1024
    spread_rows(parts_ref, weight_ref, scale_ref)

    @pl.loop(0, 1024 // TILE_L)
    def _(m):
        at = pl.ds(pl.multiple_of(base + m * TILE_L, TILE_L), TILE_L)
        to = pl.ds(pl.multiple_of(m * TILE_L, TILE_L), TILE_L)
        total = jnp.zeros((TILE_L // 8, 8, 128), F32)
        mixed = jnp.zeros((TILE_L, E), F32)
        for h, ref in enumerate(kern_refs):
            item_ref = (item_one_ref, item_two_ref)[h // 2]
            for n in range(QUART // 256):
                lanes = slice(256 * n, 256 * (n + 1))
                first = QUART * (h % 2) + 256 * n
                by = scale_ref[:, QUART * h + 256 * n : QUART * h + 256 * (n + 1)]
                block = ref[at, lanes].reshape(TILE_L // 8, 8, 256) * by[None]
                total = total + block[:, :, :128] + block[:, :, 128:]
                block = block.reshape(TILE_L, 256).astype(BF16)
                mixed = mixed + jnp.dot(block, item_ref[first : first + 256, :], preferred_element_type=F32)
        partial_ref[to, :] = total.reshape(TILE_L, 128)
        out_ref[to, :] = mixed.astype(BF16)

    cols = lanes_of(partial_ref[...])
    high = cols.astype(BF16).astype(F32)
    both = jnp.concatenate([high, cols - high], 1)
    for q in range(4):
        block = jnp.concatenate([both[2 * q : 2 * q + 2], jnp.zeros((14, E), F32)], 0)
        out_ref[1024 + 16 * q : 1024 + 16 * (q + 1), :] = block.astype(BF16)


def last_pass(other, kern, item, parts, weight):
    return call(
        functools.partial(last_body, other), (*kern, *item, parts, weight), VMEM((1088, E), BF16),
        [VMEM((8, ITEM_DEV), F32), VMEM((1024, 128), F32)], "totals", LIST_DEV * ITEM_DEV * E, 4,
    )


AWAY = (0, 1, 3, 2)


def fold_body(stay_ref, came_ref, *out_refs):
    _, z, _, _ = place()
    for d, out_ref in zip(AWAY, out_refs):
        q = (z + d) % 4
        rows = pl.ds(pl.multiple_of(q * 256, 256), 256)
        tail = pl.ds(pl.multiple_of(1024 + q * 16, 16), 16)
        out_ref[:256, :] = (stay_ref[rows, :].astype(F32) + came_ref[rows, :].astype(F32)).astype(out_ref.dtype)
        cols = stay_ref[tail, :].astype(F32) + came_ref[tail, :].astype(F32)
        cols = cols[:, :128] + cols[:, 128:]
        high = cols.astype(BF16).astype(F32)
        out_ref[256:, :] = jnp.concatenate([high, cols - high], 1).astype(out_ref.dtype)


def fold(stay, came):
    out = (VMEM((272, E), F32),) + (VMEM((272, E), BF16),) * 3
    return call(fold_body, (stay, came), out, [], "fold")


def finish_body(mine_ref, a_ref, b_ref, c_ref, list_ref, out_ref):
    core, z, _, _ = place()
    first = pl.multiple_of(core * 1024 + z * 256, 256)
    totals = mine_ref[...] + a_ref[...].astype(F32) + b_ref[...].astype(F32) + c_ref[...].astype(F32)
    cols = totals[256:, :128] + totals[256:, 128:]
    for t in range(2):
        col = jnp.broadcast_to(cols[t : t + 1], (128, 128)).T
        col = jnp.concatenate([col, col], 1)
        own = list_ref[pl.ds(first + 128 * t, 128), :].astype(F32)
        mixed = 0.1 * own + totals[128 * t : 128 * (t + 1)] / col
        out_ref[128 * t : 128 * (t + 1), :] = unit(mixed, 1).astype(BF16)


def finish(pieces, lists):
    return call(finish_body, (*pieces, lists), VMEM((256, E), BF16), [], "finish")


FROM = (0, -1, 1, 2)


def lay_body(*refs):
    blocks, out_ref, sems = refs[:8], refs[8], refs[9]
    core, z, _, _ = place()
    copies = []
    for i, ref in enumerate(blocks):
        half = core if i < 4 else 1 - core
        row = pl.multiple_of(half * 1024 + (z + FROM[i % 4] + 4) % 4 * 256, 256)
        copies.append(pltpu.make_async_copy(ref, out_ref.at[pl.ds(row, 256), :], sems.at[i]))
    for copy in copies:
        copy.start()
    for copy in copies:
        copy.wait()


def lay(blocks):
    return pl.pallas_call(
        lay_body,
        out_shape=jax.ShapeDtypeStruct((LIST_DEV, E), BF16),
        in_specs=whole(8),
        out_specs=pl.BlockSpec(memory_space=pl.ANY),
        scratch_shapes=[pltpu.SemaphoreType.DMA((8,))],
        compiler_params=pltpu.CompilerParams(vmem_limit_bytes=12 << 20),
        name="lay",
    )(*blocks)


def local(items, item_weight, list_capacity, centroids):
    feat = items.T
    weight = item_weight.reshape(16, 256)
    cap = list_capacity.reshape(16, 128)

    one = jnp.concatenate(gather_small(feat[:, :HALF], "x"), 0)
    two = jnp.concatenate(gather_small(feat[:, HALF:], "y"), 0)
    one = gather_large(one, "y")
    two = gather_large(two, "x")

    lists, weight, cap = prep(centroids, weight, cap)
    *kern_one, item_one, before = gen(False, lists, one)
    *kern_two, item_two, parts = gen(True, lists, two, (before,))
    kern, item = kern_one + kern_two, (item_one, item_two)

    for step in range(ITERS - 1):
        parts = lax.all_to_all(parts, "list", 0, 0)
        cols = lax.all_to_all(col_pass(kern, parts, weight), "item", 0, 0)
        parts = row_pass(kern, cols, cap)
    parts = lax.all_to_all(parts, "list", 0, 0)

    came = swap_core(last_pass(True, kern, item, parts, weight))
    stay = last_pass(False, kern, item, parts, weight)
    pieces = fold(stay, came)
    pieces = pieces[:1] + tuple(shift("z", d)(p) for d, p in zip(AWAY[1:], pieces[1:]))
    done = finish(pieces, lists)
    done = [done] + [shift("z", d)(done) for d in AWAY[1:]]
    return lay(done + [swap_core(d) for d in done])


def solution(mesh):
    placed = (P("item", "list"), P("item"), P("list"), P("list", None))
    return jax.shard_map(
        local, mesh=mesh, in_specs=placed, out_specs=P("list", None), check_vma=False
    )
```

```python
import functools
import math

import jax
import jax.numpy as jnp
from jax import lax
from jax.experimental import pallas as pl
from jax.experimental.pallas import tpu as pltpu
from jax.sharding import PartitionSpec as P

E = 256
ITERS = 3
EPS = 1e-06
SHARP = 2.5 * math.sqrt(E) * math.log2(math.e)

ITEM_DEV = 4096
LIST_DEV = 2048
QUART = ITEM_DEV // 4
N_ITEM = 8
N_LIST = 16

F32 = jnp.float32
BF16 = jnp.bfloat16
VMEM = pltpu.VMEM


def whole(n):
    return [pl.BlockSpec(memory_space=VMEM)] * n


def call(body, args, out, scratch, name, flops=0, limit=4):
    return pl.pallas_call(
        body,
        out_shape=out,
        in_specs=whole(len(args)),
        out_specs=tuple(whole(len(out))) if isinstance(out, tuple) else whole(1)[0],
        scratch_shapes=scratch,
        compiler_params=pltpu.CompilerParams(vmem_limit_bytes=limit << 20),
        cost_estimate=pl.CostEstimate(flops=flops, bytes_accessed=1 << 20, transcendentals=0),
        name=name,
    )(*args)


def unit(values, axis):
    square = jnp.mean(values * values, axis=axis, keepdims=True)
    return values * lax.rsqrt(square + EPS) * E ** (-0.5)


def place():
    item = lax.axis_index("item")
    spot = lax.axis_index("list")
    return item % 2, item // 2, spot // 4, spot % 4


def shift_z(block, step):
    return lax.ppermute(block, "item", [(i, (i + 2 * step) % N_ITEM) for i in range(N_ITEM)])


def swap_core(block):
    return lax.ppermute(block, "item", [(i, i ^ 1) for i in range(N_ITEM)])


def shift_plane(block, first, step):
    pairs = []
    for i in range(N_ITEM):
        for spot in range(N_LIST):
            if (i % 2 == 0) == first:
                to = spot // 4 * 4 + (spot + step) % 4
            else:
                to = (spot + 4 * step) % N_LIST
            pairs.append((i * N_LIST + spot, i * N_LIST + to))
    return lax.ppermute(block, ("item", "list"), pairs)


ORDER = (0, -1, 1, 2)


def gather(feat):
    block = jnp.concatenate([feat] + [shift_plane(feat, True, d) for d in (1, 3, 2)], 0)
    left, right = shift_plane(block, False, 1), shift_plane(block, False, 3)
    n = block.shape[0] // 2
    return [block, left, right, shift_plane(left[:n], False, 1), shift_plane(right[n:], False, 3)]


def prep_body(cent_ref, list_ref, raw_ref, sems):
    parts = [pl.ds(512 * m, 512) for m in range(4)]
    copies = [pltpu.make_async_copy(cent_ref.at[p, :], raw_ref.at[p, :], sems.at[m]) for m, p in enumerate(parts)]
    for copy in copies:
        copy.start()
    for copy, p in zip(copies, parts):
        copy.wait()
        list_ref[p, :] = unit(raw_ref[p, :].astype(F32), 1).astype(BF16)


def prep(cent):
    return pl.pallas_call(
        prep_body,
        out_shape=VMEM((LIST_DEV, E), BF16),
        in_specs=[pl.BlockSpec(memory_space=pl.ANY)],
        out_specs=whole(1)[0],
        scratch_shapes=[VMEM((LIST_DEV, E), BF16), pltpu.SemaphoreType.DMA((4,))],
        compiler_params=pltpu.CompilerParams(vmem_limit_bytes=4 << 20),
        name="lists",
    )(cent)


def put_rows(total, out_ref):
    rows = jnp.concatenate([total[:, 128 * k : 128 * (k + 1)] for k in range(32)], 0)
    out_ref[...] = jnp.broadcast_to(rows.astype(BF16)[None], (N_LIST, 32, 128))


TILE_M = 256


def gen_body(list_ref, own_ref, left_ref, right_ref, low_ref, high_ref, *refs):
    *kern_refs, item_ref, rows_ref, feat_ref = refs
    core, _, y, x = place()
    for i, outer in enumerate(ORDER):
        for j, inner in enumerate(ORDER):
            if i < 3:
                block = (own_ref, left_ref, right_ref)[i][16 * j : 16 * (j + 1), :]
            else:
                block = (low_ref, high_ref)[j // 2][16 * (j % 2) : 16 * (j % 2 + 1), :]
            from_y = (y + jnp.where(core == 0, outer, inner) + 4) % 4
            from_x = (x + jnp.where(core == 0, inner, outer) + 4) % 4
            spot = from_y * 4 + from_x
            feat_ref[pl.ds(pl.multiple_of(spot * 16, 16), 16), :] = block

    totals = []
    for n, kern_ref in enumerate(kern_refs):
        at = slice(QUART * n, QUART * (n + 1))
        block = feat_ref[:, at]
        wide = block.astype(F32)
        norm = lax.rsqrt(jnp.mean(wide * wide, axis=0, keepdims=True) + EPS) * E ** (-0.5)
        item_ref[at, :] = (wide * norm).T.astype(BF16)
        norm = norm * SHARP
        total = jnp.zeros((8, QUART), F32)
        for m in range(LIST_DEV // TILE_M):
            rows = slice(TILE_M * m, TILE_M * (m + 1))
            score = jnp.dot(list_ref[rows, :], block, preferred_element_type=F32)
            value = jnp.exp2(score * norm)
            kern_ref[rows, :] = value
            total = total + value.reshape(TILE_M // 8, 8, QUART).sum(0)
        totals.append(total.sum(0, keepdims=True))
    put_rows(jnp.concatenate(totals, 1), rows_ref)


def gen(lists, pieces):
    out = (VMEM((LIST_DEV, QUART), F32),) * 4 + (VMEM((ITEM_DEV, E), BF16), VMEM((N_LIST, 32, 128), BF16))
    return call(gen_body, (lists, *pieces), out, [VMEM((E, ITEM_DEV), BF16)], "generate", 2 * LIST_DEV * ITEM_DEV * E, 8)


def spread_rows(parts_ref, weight_ref, scale_ref):
    scale = weight_ref[...] / parts_ref[...].astype(F32).sum(0)
    for k in range(32):
        scale_ref[:, 128 * k : 128 * (k + 1)] = jnp.broadcast_to(scale[k : k + 1, :], (8, 128))


def lane(partial):
    return partial.T.sum(0, keepdims=True)


def col_body(*refs):
    *kern_refs, parts_ref, weight_ref, out_ref, scale_ref = refs
    spread_rows(parts_ref, weight_ref, scale_ref)
    cols = []
    for m in range(LIST_DEV // 128):
        at = slice(128 * m, 128 * (m + 1))
        total = jnp.zeros((16, 8, 128), F32)
        for h, ref in enumerate(kern_refs):
            for n in range(QUART // 128):
                by = scale_ref[:, QUART * h + 128 * n : QUART * h + 128 * (n + 1)]
                total = total + ref[at, 128 * n : 128 * (n + 1)].reshape(16, 8, 128) * by[None]
        cols.append(lane(total.reshape(128, 128)))
    out_ref[...] = jnp.broadcast_to(jnp.concatenate(cols, 0)[None], (N_ITEM, 16, 128))


def col_pass(kern, parts, weight):
    return call(
        col_body, (*kern, parts, weight), VMEM((N_ITEM, 16, 128), F32), [VMEM((8, ITEM_DEV), F32)],
        "columns", 2 * LIST_DEV * ITEM_DEV,
    )


def row_body(*refs):
    *kern_refs, cols_ref, cap_ref, out_ref, scale_ref, total_ref = refs
    scale = cap_ref[...] / cols_ref[...].sum(0)
    for k in range(16):
        scale_ref[128 * k : 128 * (k + 1), :] = jnp.broadcast_to(scale[k : k + 1, :], (128, 128)).T

    for h, ref in enumerate(kern_refs):

        def step(m, total):
            at = pl.ds(pl.multiple_of(m * 128, 128), 128)
            by = scale_ref[at, :].reshape(16, 8, 128)
            block = ref[at, :].reshape(16, 8, QUART)
            total = list(total)
            for j in range(16):
                for k in range(8):
                    total[k] = total[k] + block[j, :, 128 * k : 128 * (k + 1)] * by[j]
            return tuple(total)

        total = lax.fori_loop(0, LIST_DEV // 128, step, (jnp.zeros((8, 128), F32),) * 8)
        for k in range(8):
            first = QUART * h + 128 * k
            total_ref[:, first : first + 128] = total[k].sum(0, keepdims=True)

    put_rows(total_ref[...], out_ref)


def row_pass(kern, cols, cap):
    return call(
        row_body, (*kern, cols, cap), VMEM((N_LIST, 32, 128), BF16),
        [VMEM((LIST_DEV, 128), F32), VMEM((1, ITEM_DEV), F32)], "rows", 2 * LIST_DEV * ITEM_DEV,
    )


TILE_L = 256


def last_body(other, *refs):
    *kern_refs, item_ref, parts_ref, weight_ref, out_ref, scale_ref = refs
    core, _, _, _ = place()
    base = (1 - core if other else core) * 1024
    spread_rows(parts_ref, weight_ref, scale_ref)
    cols = []
    for m in range(1024 // TILE_L):
        at = pl.ds(pl.multiple_of(base + m * TILE_L, TILE_L), TILE_L)
        total = jnp.zeros((TILE_L // 8, 8, 128), F32)
        mixed = jnp.zeros((TILE_L, E), F32)
        for h, ref in enumerate(kern_refs):
            for n in range(QUART // 256):
                first = QUART * h + 256 * n
                block = ref[at, 256 * n : 256 * (n + 1)].reshape(TILE_L // 8, 8, 256)
                block = block * scale_ref[:, first : first + 256][None]
                total = total + block[:, :, :128] + block[:, :, 128:]
                block = block.reshape(TILE_L, 256).astype(BF16)
                mixed = mixed + jnp.dot(block, item_ref[first : first + 256, :], preferred_element_type=F32)
        out_ref[TILE_L * m : TILE_L * (m + 1), :] = mixed.astype(BF16)
        total = total.reshape(TILE_L, 128)
        cols += [lane(total[128 * t : 128 * (t + 1)]) for t in range(TILE_L // 128)]

    for q in range(4):
        col = jnp.concatenate(cols[2 * q : 2 * q + 2], 0)
        high = col.astype(BF16).astype(F32)
        block = jnp.concatenate([jnp.concatenate([high, col - high], 1), jnp.zeros((14, E), F32)], 0)
        out_ref[1024 + 16 * q : 1024 + 16 * (q + 1), :] = block.astype(BF16)


def last_pass(other, kern, item, parts, weight):
    return call(
        functools.partial(last_body, other), (*kern, item, parts, weight), VMEM((1088, E), BF16),
        [VMEM((8, ITEM_DEV), F32)], "totals", LIST_DEV * ITEM_DEV * E, 4,
    )


AWAY = (0, 1, 3, 2)


def fold_body(stay_ref, came_ref, *out_refs):
    _, z, _, _ = place()
    for d, out_ref in zip(AWAY, out_refs):
        q = (z + d) % 4
        rows = pl.ds(pl.multiple_of(q * 256, 256), 256)
        tail = pl.ds(pl.multiple_of(1024 + q * 16, 16), 16)
        out_ref[:256, :] = (stay_ref[rows, :].astype(F32) + came_ref[rows, :].astype(F32)).astype(out_ref.dtype)
        cols = stay_ref[tail, :].astype(F32) + came_ref[tail, :].astype(F32)
        cols = cols[:, :128] + cols[:, 128:]
        high = cols.astype(BF16).astype(F32)
        out_ref[256:, :] = jnp.concatenate([high, cols - high], 1).astype(out_ref.dtype)


def fold(stay, came):
    out = (VMEM((272, E), F32),) + (VMEM((272, E), BF16),) * 3
    return call(fold_body, (stay, came), out, [], "fold")


def finish_body(mine_ref, a_ref, b_ref, c_ref, list_ref, out_ref):
    core, z, _, _ = place()
    first = pl.multiple_of(core * 1024 + z * 256, 256)
    totals = mine_ref[...] + a_ref[...].astype(F32) + b_ref[...].astype(F32) + c_ref[...].astype(F32)
    cols = totals[256:, :128] + totals[256:, 128:]
    for t in range(2):
        col = jnp.broadcast_to(cols[t : t + 1], (128, 128)).T
        col = jnp.concatenate([col, col], 1)
        own = list_ref[pl.ds(first + 128 * t, 128), :].astype(F32)
        mixed = 0.1 * own + totals[128 * t : 128 * (t + 1)] / col
        out_ref[128 * t : 128 * (t + 1), :] = unit(mixed, 1).astype(BF16)


def finish(pieces, lists):
    return call(finish_body, (*pieces, lists), VMEM((256, E), BF16), [], "finish")


FROM = (0, -1, 1, 2)


def lay_body(*refs):
    blocks, out_ref, sems = refs[:8], refs[8], refs[9]
    core, z, _, _ = place()
    copies = []
    for i, ref in enumerate(blocks):
        half = core if i < 4 else 1 - core
        row = pl.multiple_of(half * 1024 + (z + FROM[i % 4] + 4) % 4 * 256, 256)
        copies.append(pltpu.make_async_copy(ref, out_ref.at[pl.ds(row, 256), :], sems.at[i]))
    for copy in copies:
        copy.start()
    for copy in copies:
        copy.wait()


def lay(blocks):
    return pl.pallas_call(
        lay_body,
        out_shape=jax.ShapeDtypeStruct((LIST_DEV, E), BF16),
        in_specs=whole(8),
        out_specs=pl.BlockSpec(memory_space=pl.ANY),
        scratch_shapes=[pltpu.SemaphoreType.DMA((8,))],
        compiler_params=pltpu.CompilerParams(vmem_limit_bytes=12 << 20),
        name="lay",
    )(*blocks)


def local(items, item_weight, list_capacity, centroids):
    weight = item_weight.reshape(32, 128)
    cap = list_capacity.reshape(16, 128)
    lists = prep(centroids)
    *kern, item, parts = gen(lists, gather(items.T))

    for step in range(ITERS - 1):
        parts = lax.all_to_all(parts, "list", 0, 0)
        cols = lax.all_to_all(col_pass(kern, parts, weight), "item", 0, 0)
        parts = row_pass(kern, cols, cap)
    parts = lax.all_to_all(parts, "list", 0, 0)

    came = swap_core(last_pass(True, kern, item, parts, weight))
    stay = last_pass(False, kern, item, parts, weight)
    pieces = fold(stay, came)
    pieces = pieces[:1] + tuple(shift_z(p, d) for d, p in zip(AWAY[1:], pieces[1:]))
    done = finish(pieces, lists)
    done = [done] + [shift_z(done, d) for d in AWAY[1:]]
    return lay(done + [swap_core(d) for d in done])


def solution(mesh):
    placed = (P("item", "list"), P("item"), P("list"), P("list", None))
    return jax.shard_map(
        local, mesh=mesh, in_specs=placed, out_specs=P("list", None), check_vma=False
    )
```

```python
import functools
import math

import jax
import jax.numpy as jnp
from jax import lax
from jax.experimental import pallas as pl
from jax.experimental.pallas import tpu as pltpu
from jax.sharding import PartitionSpec as P

E = 256
ITERS = 3
EPS = 1e-06
SHARP = 2.5 * math.sqrt(E) * math.log2(math.e)

ITEM_DEV = 4096
LIST_DEV = 2048
QUART = ITEM_DEV // 4
N_ITEM = 8
N_LIST = 16

F32 = jnp.float32
BF16 = jnp.bfloat16
VMEM = pltpu.VMEM


def whole(n):
    return [pl.BlockSpec(memory_space=VMEM)] * n


def call(body, args, out, scratch, name, flops=0, limit=4):
    return pl.pallas_call(
        body,
        out_shape=out,
        in_specs=whole(len(args)),
        out_specs=tuple(whole(len(out))) if isinstance(out, tuple) else whole(1)[0],
        scratch_shapes=scratch,
        compiler_params=pltpu.CompilerParams(vmem_limit_bytes=limit << 20),
        cost_estimate=pl.CostEstimate(flops=flops, bytes_accessed=1 << 20, transcendentals=0),
        name=name,
    )(*args)


def unit(values, axis):
    square = jnp.mean(values * values, axis=axis, keepdims=True)
    return values * lax.rsqrt(square + EPS) * E ** (-0.5)


def place():
    item = lax.axis_index("item")
    spot = lax.axis_index("list")
    return item % 2, item // 2, spot // 4, spot % 4


def shift_z(block, step):
    return lax.ppermute(block, "item", [(i, (i + 2 * step) % N_ITEM) for i in range(N_ITEM)])


def swap_core(block):
    return lax.ppermute(block, "item", [(i, i ^ 1) for i in range(N_ITEM)])


def shift_plane(block, first, step):
    pairs = []
    for i in range(N_ITEM):
        for spot in range(N_LIST):
            if (i % 2 == 0) == first:
                to = spot // 4 * 4 + (spot + step) % 4
            else:
                to = (spot + 4 * step) % N_LIST
            pairs.append((i * N_LIST + spot, i * N_LIST + to))
    return lax.ppermute(block, ("item", "list"), pairs)


ORDER = (0, -1, 1, 2)


def gather(feat, own):
    came = [shift_plane(feat, True, d) for d in (1, 3, 2)]
    low, high = jnp.concatenate([own, came[0]], 0), jnp.concatenate(came[1:], 0)
    left_low, right_high = shift_plane(low, False, 1), shift_plane(high, False, 3)
    left_high, right_low = shift_plane(high, False, 1), shift_plane(low, False, 3)
    far = [shift_plane(left_low, False, 1), shift_plane(right_high, False, 3)]
    return [low, high, left_low, left_high, right_low, right_high] + far


def prep_body(cent_ref, feat_ref, list_ref, own_ref, raw_ref, sems):
    parts = [pl.ds(512 * m, 512) for m in range(4)]
    copies = [pltpu.make_async_copy(cent_ref.at[p, :], raw_ref.at[p, :], sems.at[m]) for m, p in enumerate(parts)]
    copies.append(pltpu.make_async_copy(feat_ref, own_ref, sems.at[4]))
    for copy in copies:
        copy.start()
    for copy, p in zip(copies, parts):
        copy.wait()
        list_ref[p, :] = unit(raw_ref[p, :].astype(F32), 1).astype(BF16)
    copies[4].wait()


def prep(cent, feat):
    return pl.pallas_call(
        prep_body,
        out_shape=(VMEM((LIST_DEV, E), BF16), VMEM(feat.shape, BF16)),
        in_specs=[pl.BlockSpec(memory_space=pltpu.HBM)] * 2,
        out_specs=tuple(whole(2)),
        scratch_shapes=[VMEM((LIST_DEV, E), BF16), pltpu.SemaphoreType.DMA((5,))],
        compiler_params=pltpu.CompilerParams(vmem_limit_bytes=4 << 20),
        cost_estimate=pl.CostEstimate(flops=1 << 20, bytes_accessed=1 << 21, transcendentals=0),
        name="lists",
    )(cent, feat)


def put_rows(total, out_ref):
    rows = jnp.concatenate([total[:, 128 * k : 128 * (k + 1)] for k in range(32)], 0)
    out_ref[...] = jnp.broadcast_to(rows.astype(BF16)[None], (N_LIST, 32, 128))


TILE_M = 256


def gen_body(list_ref, *refs):
    piece_refs, (*kern_refs, item_ref, rows_ref, feat_ref) = refs[:8], refs[8:]
    core, _, y, x = place()
    for i, outer in enumerate(ORDER):
        for j, inner in enumerate(ORDER):
            block = piece_refs[2 * i + j // 2][16 * (j % 2) : 16 * (j % 2 + 1), :]
            from_y = (y + jnp.where(core == 0, outer, inner) + 4) % 4
            from_x = (x + jnp.where(core == 0, inner, outer) + 4) % 4
            spot = from_y * 4 + from_x
            feat_ref[pl.ds(pl.multiple_of(spot * 16, 16), 16), :] = block

    totals = []
    for n, kern_ref in enumerate(kern_refs):
        at = slice(QUART * n, QUART * (n + 1))
        block = feat_ref[:, at]
        wide = block.astype(F32)
        norm = lax.rsqrt(jnp.mean(wide * wide, axis=0, keepdims=True) + EPS) * E ** (-0.5)
        item_ref[at, :] = (wide * norm).T.astype(BF16)
        norm = norm * SHARP
        total = jnp.zeros((8, QUART), F32)
        for m in range(LIST_DEV // TILE_M):
            rows = slice(TILE_M * m, TILE_M * (m + 1))
            score = jnp.dot(list_ref[rows, :], block, preferred_element_type=F32)
            value = jnp.exp2(score * norm)
            kern_ref[rows, :] = value
            total = total + value.reshape(TILE_M // 8, 8, QUART).sum(0)
        totals.append(total.sum(0, keepdims=True))
    put_rows(jnp.concatenate(totals, 1), rows_ref)


def gen(lists, pieces):
    out = (VMEM((LIST_DEV, QUART), F32),) * 4 + (VMEM((ITEM_DEV, E), BF16), VMEM((N_LIST, 32, 128), BF16))
    return call(gen_body, (lists, *pieces), out, [VMEM((E, ITEM_DEV), BF16)], "generate", 2 * LIST_DEV * ITEM_DEV * E, 8)


def spread_rows(parts_ref, weight_ref, scale_ref):
    scale = weight_ref[...] / parts_ref[...].astype(F32).sum(0)
    for k in range(32):
        scale_ref[:, 128 * k : 128 * (k + 1)] = jnp.broadcast_to(scale[k : k + 1, :], (8, 128))


def lane(partial):
    return partial.T.sum(0, keepdims=True)


def col_body(*refs):
    *kern_refs, parts_ref, weight_ref, out_ref, scale_ref = refs
    spread_rows(parts_ref, weight_ref, scale_ref)
    cols = []
    for m in range(LIST_DEV // 128):
        at = slice(128 * m, 128 * (m + 1))
        total = jnp.zeros((16, 8, 128), F32)
        for h, ref in enumerate(kern_refs):
            for n in range(QUART // 128):
                by = scale_ref[:, QUART * h + 128 * n : QUART * h + 128 * (n + 1)]
                total = total + ref[at, 128 * n : 128 * (n + 1)].reshape(16, 8, 128) * by[None]
        cols.append(lane(total.reshape(128, 128)))
    out_ref[...] = jnp.broadcast_to(jnp.concatenate(cols, 0)[None], (N_ITEM, 16, 128))


def col_pass(kern, parts, weight):
    return call(
        col_body, (*kern, parts, weight), VMEM((N_ITEM, 16, 128), F32), [VMEM((8, ITEM_DEV), F32)],
        "columns", 2 * LIST_DEV * ITEM_DEV,
    )


def row_body(*refs):
    *kern_refs, cols_ref, cap_ref, out_ref, scale_ref, total_ref = refs
    scale = cap_ref[...] / cols_ref[...].sum(0)
    for k in range(16):
        scale_ref[128 * k : 128 * (k + 1), :] = jnp.broadcast_to(scale[k : k + 1, :], (128, 128)).T

    for h, ref in enumerate(kern_refs):

        def step(m, total):
            at = pl.ds(pl.multiple_of(m * 128, 128), 128)
            by = scale_ref[at, :].reshape(16, 8, 128)
            block = ref[at, :].reshape(16, 8, QUART)
            total = list(total)
            for j in range(16):
                for k in range(8):
                    total[k] = total[k] + block[j, :, 128 * k : 128 * (k + 1)] * by[j]
            return tuple(total)

        total = lax.fori_loop(0, LIST_DEV // 128, step, (jnp.zeros((8, 128), F32),) * 8)
        for k in range(8):
            first = QUART * h + 128 * k
            total_ref[:, first : first + 128] = total[k].sum(0, keepdims=True)

    put_rows(total_ref[...], out_ref)


def row_pass(kern, cols, cap):
    return call(
        row_body, (*kern, cols, cap), VMEM((N_LIST, 32, 128), BF16),
        [VMEM((LIST_DEV, 128), F32), VMEM((1, ITEM_DEV), F32)], "rows", 2 * LIST_DEV * ITEM_DEV,
    )


TILE_L = 256


def last_body(other, *refs):
    *kern_refs, item_ref, parts_ref, weight_ref, out_ref, scale_ref = refs
    core, _, _, _ = place()
    base = (1 - core if other else core) * 1024
    spread_rows(parts_ref, weight_ref, scale_ref)
    cols = []
    for m in range(1024 // TILE_L):
        at = pl.ds(pl.multiple_of(base + m * TILE_L, TILE_L), TILE_L)
        total = jnp.zeros((TILE_L // 8, 8, 128), F32)
        mixed = jnp.zeros((TILE_L, E), F32)
        for h, ref in enumerate(kern_refs):
            for n in range(QUART // 256):
                first = QUART * h + 256 * n
                block = ref[at, 256 * n : 256 * (n + 1)].reshape(TILE_L // 8, 8, 256)
                block = block * scale_ref[:, first : first + 256][None]
                total = total + block[:, :, :128] + block[:, :, 128:]
                block = block.reshape(TILE_L, 256).astype(BF16)
                mixed = mixed + jnp.dot(block, item_ref[first : first + 256, :], preferred_element_type=F32)
        out_ref[TILE_L * m : TILE_L * (m + 1), :] = mixed.astype(BF16)
        total = total.reshape(TILE_L, 128)
        cols += [lane(total[128 * t : 128 * (t + 1)]) for t in range(TILE_L // 128)]

    for q in range(4):
        col = jnp.concatenate(cols[2 * q : 2 * q + 2], 0)
        high = col.astype(BF16).astype(F32)
        block = jnp.concatenate([jnp.concatenate([high, col - high], 1), jnp.zeros((14, E), F32)], 0)
        out_ref[1024 + 16 * q : 1024 + 16 * (q + 1), :] = block.astype(BF16)


def last_pass(other, kern, item, parts, weight):
    return call(
        functools.partial(last_body, other), (*kern, item, parts, weight), VMEM((1088, E), BF16),
        [VMEM((8, ITEM_DEV), F32)], "totals", LIST_DEV * ITEM_DEV * E, 4,
    )


AWAY = (0, 1, 3, 2)


def fold_body(stay_ref, came_ref, *out_refs):
    _, z, _, _ = place()
    for d, out_ref in zip(AWAY, out_refs):
        q = (z + d) % 4
        rows = pl.ds(pl.multiple_of(q * 256, 256), 256)
        tail = pl.ds(pl.multiple_of(1024 + q * 16, 16), 16)
        out_ref[:256, :] = (stay_ref[rows, :].astype(F32) + came_ref[rows, :].astype(F32)).astype(out_ref.dtype)
        cols = stay_ref[tail, :].astype(F32) + came_ref[tail, :].astype(F32)
        cols = cols[:, :128] + cols[:, 128:]
        high = cols.astype(BF16).astype(F32)
        out_ref[256:, :] = jnp.concatenate([high, cols - high], 1).astype(out_ref.dtype)


def fold(stay, came):
    out = (VMEM((272, E), F32),) + (VMEM((272, E), BF16),) * 3
    return call(fold_body, (stay, came), out, [], "fold")


def finish_body(mine_ref, a_ref, b_ref, c_ref, list_ref, out_ref):
    core, z, _, _ = place()
    first = pl.multiple_of(core * 1024 + z * 256, 256)
    totals = mine_ref[...] + a_ref[...].astype(F32) + b_ref[...].astype(F32) + c_ref[...].astype(F32)
    cols = totals[256:, :128] + totals[256:, 128:]
    for t in range(2):
        col = jnp.broadcast_to(cols[t : t + 1], (128, 128)).T
        col = jnp.concatenate([col, col], 1)
        own = list_ref[pl.ds(first + 128 * t, 128), :].astype(F32)
        mixed = 0.1 * own + totals[128 * t : 128 * (t + 1)] / col
        out_ref[128 * t : 128 * (t + 1), :] = unit(mixed, 1).astype(BF16)


def finish(pieces, lists):
    return call(finish_body, (*pieces, lists), VMEM((256, E), BF16), [], "finish")


FROM = (0, -1, 1, 2)


def lay_body(*refs):
    blocks, out_ref, sems = refs[:8], refs[8], refs[9]
    core, z, _, _ = place()
    copies = []
    for i, ref in enumerate(blocks):
        half = core if i < 4 else 1 - core
        row = pl.multiple_of(half * 1024 + (z + FROM[i % 4] + 4) % 4 * 256, 256)
        copies.append(pltpu.make_async_copy(ref, out_ref.at[pl.ds(row, 256), :], sems.at[i]))
    for copy in copies:
        copy.start()
    for copy in copies:
        copy.wait()


def lay(blocks):
    return pl.pallas_call(
        lay_body,
        out_shape=jax.ShapeDtypeStruct((LIST_DEV, E), BF16),
        in_specs=whole(8),
        out_specs=pl.BlockSpec(memory_space=pl.ANY),
        scratch_shapes=[pltpu.SemaphoreType.DMA((8,))],
        compiler_params=pltpu.CompilerParams(vmem_limit_bytes=12 << 20),
        name="lay",
    )(*blocks)


def local(items, item_weight, list_capacity, centroids):
    weight = item_weight.reshape(32, 128)
    cap = list_capacity.reshape(16, 128)
    feat = items.T
    lists, own = prep(centroids, feat)
    *kern, item, parts = gen(lists, gather(feat, own))

    for step in range(ITERS - 1):
        parts = lax.all_to_all(parts, "list", 0, 0)
        cols = lax.all_to_all(col_pass(kern, parts, weight), "item", 0, 0)
        parts = row_pass(kern, cols, cap)
    parts = lax.all_to_all(parts, "list", 0, 0)

    came = swap_core(last_pass(True, kern, item, parts, weight))
    stay = last_pass(False, kern, item, parts, weight)
    pieces = fold(stay, came)
    pieces = pieces[:1] + tuple(shift_z(p, d) for d, p in zip(AWAY[1:], pieces[1:]))
    done = finish(pieces, lists)
    done = [done] + [shift_z(done, d) for d in AWAY[1:]]
    return lay(done + [swap_core(d) for d in done])


def solution(mesh):
    placed = (P("item", "list"), P("item"), P("list"), P("list", None))
    return jax.shard_map(
        local, mesh=mesh, in_specs=placed, out_specs=P("list", None), check_vma=False
    )
```

```python
import functools
import math

import jax
import jax.numpy as jnp
from jax import lax
from jax.experimental import pallas as pl
from jax.experimental.pallas import tpu as pltpu
from jax.sharding import PartitionSpec as P

E = 256
ITERS = 3
EPS = 1e-06
SHARP = 2.5 * math.sqrt(E) * math.log2(math.e)

ITEM_DEV = 4096
LIST_DEV = 2048
QUART = ITEM_DEV // 4
N_ITEM = 8
N_LIST = 16

F32 = jnp.float32
BF16 = jnp.bfloat16
VMEM = pltpu.VMEM


def whole(n):
    return [pl.BlockSpec(memory_space=VMEM)] * n


def call(body, args, out, scratch, name, flops=0, limit=4):
    return pl.pallas_call(
        body,
        out_shape=out,
        in_specs=whole(len(args)),
        out_specs=tuple(whole(len(out))) if isinstance(out, tuple) else whole(1)[0],
        scratch_shapes=scratch,
        compiler_params=pltpu.CompilerParams(vmem_limit_bytes=limit << 20),
        cost_estimate=pl.CostEstimate(flops=flops, bytes_accessed=1 << 20, transcendentals=0),
        name=name,
    )(*args)


def unit(values, axis):
    square = jnp.mean(values * values, axis=axis, keepdims=True)
    return values * lax.rsqrt(square + EPS) * E ** (-0.5)


def place():
    item = lax.axis_index("item")
    spot = lax.axis_index("list")
    return item % 2, item // 2, spot // 4, spot % 4


def swap_core(block):
    return lax.ppermute(block, "item", [(i, i ^ 1) for i in range(N_ITEM)])


def shift_plane(block, first, step):
    pairs = []
    for i in range(N_ITEM):
        for spot in range(N_LIST):
            if (i % 2 == 0) == first:
                to = spot // 4 * 4 + (spot + step) % 4
            else:
                to = (spot + 4 * step) % N_LIST
            pairs.append((i * N_LIST + spot, i * N_LIST + to))
    return lax.ppermute(block, ("item", "list"), pairs)


ORDER = (0, -1, 1, 2)


def gather(feat, own):
    came = [shift_plane(feat, True, d) for d in (1, 3, 2)]
    low, high = jnp.concatenate([own, came[0]], 0), jnp.concatenate(came[1:], 0)
    left_low, right_high = shift_plane(low, False, 1), shift_plane(high, False, 3)
    left_high, right_low = shift_plane(high, False, 1), shift_plane(low, False, 3)
    far = [shift_plane(left_low, False, 1), shift_plane(right_high, False, 3)]
    return [low, high, left_low, left_high, right_low, right_high] + far


def prep_body(cent_ref, feat_ref, list_ref, own_ref, raw_ref, sems):
    parts = [pl.ds(512 * m, 512) for m in range(4)]
    copies = [pltpu.make_async_copy(cent_ref.at[p, :], raw_ref.at[p, :], sems.at[m]) for m, p in enumerate(parts)]
    copies.append(pltpu.make_async_copy(feat_ref, own_ref, sems.at[4]))
    for copy in copies:
        copy.start()
    for copy, p in zip(copies, parts):
        copy.wait()
        list_ref[p, :] = unit(raw_ref[p, :].astype(F32), 1).astype(BF16)
    copies[4].wait()


def prep(cent, feat):
    return pl.pallas_call(
        prep_body,
        out_shape=(VMEM((LIST_DEV, E), BF16), VMEM(feat.shape, BF16)),
        in_specs=[pl.BlockSpec(memory_space=pltpu.HBM)] * 2,
        out_specs=tuple(whole(2)),
        scratch_shapes=[VMEM((LIST_DEV, E), BF16), pltpu.SemaphoreType.DMA((5,))],
        compiler_params=pltpu.CompilerParams(vmem_limit_bytes=4 << 20),
        cost_estimate=pl.CostEstimate(flops=1 << 20, bytes_accessed=1 << 21, transcendentals=0),
        name="lists",
    )(cent, feat)


def put_rows(total, out_ref):
    rows = jnp.concatenate([total[:, 128 * k : 128 * (k + 1)] for k in range(32)], 0)
    out_ref[...] = jnp.broadcast_to(rows.astype(BF16)[None], (N_LIST, 32, 128))


TILE_M = 256


def gen_body(list_ref, *refs):
    piece_refs, (*kern_refs, item_ref, rows_ref, feat_ref) = refs[:8], refs[8:]
    core, _, y, x = place()
    for i, outer in enumerate(ORDER):
        for j, inner in enumerate(ORDER):
            block = piece_refs[2 * i + j // 2][16 * (j % 2) : 16 * (j % 2 + 1), :]
            from_y = (y + jnp.where(core == 0, outer, inner) + 4) % 4
            from_x = (x + jnp.where(core == 0, inner, outer) + 4) % 4
            spot = from_y * 4 + from_x
            feat_ref[pl.ds(pl.multiple_of(spot * 16, 16), 16), :] = block

    totals = []
    for n, kern_ref in enumerate(kern_refs):
        at = slice(QUART * n, QUART * (n + 1))
        block = feat_ref[:, at]
        wide = block.astype(F32)
        norm = lax.rsqrt(jnp.mean(wide * wide, axis=0, keepdims=True) + EPS) * E ** (-0.5)
        item_ref[at, :] = (wide * norm).T.astype(BF16)
        norm = norm * SHARP
        total = jnp.zeros((8, QUART), F32)
        for m in range(LIST_DEV // TILE_M):
            rows = slice(TILE_M * m, TILE_M * (m + 1))
            score = jnp.dot(list_ref[rows, :], block, preferred_element_type=F32)
            value = jnp.exp2(score * norm)
            kern_ref[rows, :] = value
            total = total + value.reshape(TILE_M // 8, 8, QUART).sum(0)
        totals.append(total.sum(0, keepdims=True))
    put_rows(jnp.concatenate(totals, 1), rows_ref)


def gen(lists, pieces):
    out = (VMEM((LIST_DEV, QUART), F32),) * 4 + (VMEM((ITEM_DEV, E), BF16), VMEM((N_LIST, 32, 128), BF16))
    return call(gen_body, (lists, *pieces), out, [VMEM((E, ITEM_DEV), BF16)], "generate", 2 * LIST_DEV * ITEM_DEV * E, 8)


def spread_rows(parts_ref, weight_ref, scale_ref):
    scale = weight_ref[...] / parts_ref[...].astype(F32).sum(0)
    for k in range(32):
        scale_ref[:, 128 * k : 128 * (k + 1)] = jnp.broadcast_to(scale[k : k + 1, :], (8, 128))


def lane(partial):
    return partial.T.sum(0, keepdims=True)


def col_body(*refs):
    *kern_refs, parts_ref, weight_ref, out_ref, scale_ref = refs
    spread_rows(parts_ref, weight_ref, scale_ref)
    cols = []
    for m in range(LIST_DEV // 128):
        at = slice(128 * m, 128 * (m + 1))
        total = jnp.zeros((16, 8, 128), F32)
        for h, ref in enumerate(kern_refs):
            for n in range(QUART // 128):
                by = scale_ref[:, QUART * h + 128 * n : QUART * h + 128 * (n + 1)]
                total = total + ref[at, 128 * n : 128 * (n + 1)].reshape(16, 8, 128) * by[None]
        cols.append(lane(total.reshape(128, 128)))
    out_ref[...] = jnp.broadcast_to(jnp.concatenate(cols, 0)[None], (N_ITEM, 16, 128))


def col_pass(kern, parts, weight):
    return call(
        col_body, (*kern, parts, weight), VMEM((N_ITEM, 16, 128), F32), [VMEM((8, ITEM_DEV), F32)],
        "columns", 2 * LIST_DEV * ITEM_DEV,
    )


def row_body(*refs):
    *kern_refs, cols_ref, cap_ref, out_ref, scale_ref, total_ref = refs
    scale = cap_ref[...] / cols_ref[...].sum(0)
    for k in range(16):
        scale_ref[128 * k : 128 * (k + 1), :] = jnp.broadcast_to(scale[k : k + 1, :], (128, 128)).T

    for h, ref in enumerate(kern_refs):

        def step(m, total):
            at = pl.ds(pl.multiple_of(m * 128, 128), 128)
            by = scale_ref[at, :].reshape(16, 8, 128)
            block = ref[at, :].reshape(16, 8, QUART)
            total = list(total)
            for j in range(16):
                for k in range(8):
                    total[k] = total[k] + block[j, :, 128 * k : 128 * (k + 1)] * by[j]
            return tuple(total)

        total = lax.fori_loop(0, LIST_DEV // 128, step, (jnp.zeros((8, 128), F32),) * 8)
        for k in range(8):
            first = QUART * h + 128 * k
            total_ref[:, first : first + 128] = total[k].sum(0, keepdims=True)

    put_rows(total_ref[...], out_ref)


def row_pass(kern, cols, cap):
    return call(
        row_body, (*kern, cols, cap), VMEM((N_LIST, 32, 128), BF16),
        [VMEM((LIST_DEV, 128), F32), VMEM((1, ITEM_DEV), F32)], "rows", 2 * LIST_DEV * ITEM_DEV,
    )


QROWS = 272


def pack(mixed, col, dtype):
    high = col.astype(BF16).astype(F32)
    tail = jnp.concatenate([jnp.concatenate([high, col - high], 1), jnp.zeros((14, E), F32)], 0)
    return jnp.concatenate([mixed, tail], 0).astype(dtype)


def unpack(ref, first=0):
    block = ref[first : first + QROWS, :].astype(F32)
    return block[:256], block[256:258, :128] + block[256:258, 128:]


def quarter(kern_refs, item_ref, scale_ref, half, number):
    at = pl.ds(pl.multiple_of(half * 1024 + number * 256, 256), 256)
    total = jnp.zeros((32, 8, 128), F32)
    mixed = jnp.zeros((256, E), F32)
    for h, ref in enumerate(kern_refs):
        for n in range(QUART // 256):
            first = QUART * h + 256 * n
            block = ref[at, 256 * n : 256 * (n + 1)].reshape(32, 8, 256)
            block = block * scale_ref[:, first : first + 256][None]
            total = total + block[:, :, :128] + block[:, :, 128:]
            block = block.reshape(256, 256).astype(BF16)
            mixed = mixed + jnp.dot(block, item_ref[first : first + 256, :], preferred_element_type=F32)
    total = total.reshape(256, 128)
    return mixed, jnp.concatenate([lane(total[:128]), lane(total[128:])], 0)


def go_body(fars, new, *refs):
    if new:
        *kern_refs, item_ref, parts_ref, weight_ref, out_ref, scale_ref = refs
        spread_rows(parts_ref, weight_ref, scale_ref)
    else:
        *kern_refs, item_ref, scale_ref, _, out_ref = refs
    core, z, _, _ = place()
    for i, far in enumerate(fars):
        mixed, col = quarter(kern_refs, item_ref, scale_ref, 1 - core, (z + far) % 4)
        out_ref[QROWS * i : QROWS * (i + 1), :] = pack(mixed, col, BF16)


def go(fars, new, kern, item, *more):
    out = VMEM((QROWS * len(fars), E), BF16)
    if new:
        out = (out, VMEM((8, ITEM_DEV), F32))
    body = functools.partial(go_body, fars, new)
    return call(body, (*kern, item, *more), out, [], "totals", LIST_DEV * ITEM_DEV * E)


def stay_body(far, first, *refs):
    *kern_refs, item_ref, scale_ref, came_ref, _, out_ref = refs
    core, z, _, _ = place()
    mixed, col = quarter(kern_refs, item_ref, scale_ref, core, (z + far) % 4)
    came_mixed, came_col = unpack(came_ref, first)
    out_ref[...] = pack(mixed + came_mixed, col + came_col, out_ref.dtype)


def stay(far, first, dtype, kern, item, scale, came, after):
    body = functools.partial(stay_body, far, first)
    return call(body, (*kern, item, scale, came, after), VMEM((QROWS, E), dtype), [], "stay", LIST_DEV * ITEM_DEV * E)


def finish_body(mine_ref, a_ref, b_ref, c_ref, list_ref, out_ref):
    core, z, _, _ = place()
    first = pl.multiple_of(core * 1024 + z * 256, 256)
    totals, cols = (sum(parts) for parts in zip(*(unpack(ref) for ref in (mine_ref, a_ref, b_ref, c_ref))))
    for t in range(2):
        col = jnp.broadcast_to(cols[t : t + 1], (128, 128)).T
        col = jnp.concatenate([col, col], 1)
        own = list_ref[pl.ds(first + 128 * t, 128), :].astype(F32)
        mixed = 0.1 * own + totals[128 * t : 128 * (t + 1)] / col
        out_ref[128 * t : 128 * (t + 1), :] = unit(mixed, 1).astype(BF16)


def finish(mine, came, lists):
    return call(finish_body, (mine, *came, lists), VMEM((256, E), BF16), [], "finish")


def shift_z(block, step):
    return lax.ppermute(block, "item", [(i, (i + 2 * step) % N_ITEM) for i in range(N_ITEM)])


def lay_body(spots, more, *refs):
    blocks, (out_ref, sems) = refs[more:-2], refs[-2:]
    core, z, _, _ = place()
    copies = []
    for i, ((back, other), ref) in enumerate(zip(spots, blocks)):
        half = 1 - core if other else core
        row = pl.multiple_of(half * 1024 + (z - back + 4) % 4 * 256, 256)
        copies.append(pltpu.make_async_copy(ref, out_ref.at[pl.ds(row, 256), :], sems.at[i]))
    for copy in copies:
        copy.start()
    for copy in copies:
        copy.wait()


def lay(spots, blocks, out=None):
    n = len(spots)
    more = int(out is not None)
    place_any = pl.BlockSpec(memory_space=pl.ANY)
    return pl.pallas_call(
        functools.partial(lay_body, spots, more),
        out_shape=jax.ShapeDtypeStruct((LIST_DEV, E), BF16),
        in_specs=[place_any] * more + whole(n),
        out_specs=place_any,
        input_output_aliases={0: 0} if more else {},
        scratch_shapes=[pltpu.SemaphoreType.DMA((n,))],
        compiler_params=pltpu.CompilerParams(vmem_limit_bytes=4 << 20),
        name="lay",
    )(*([out] if more else []), *blocks)


def local(items, item_weight, list_capacity, centroids):
    weight = item_weight.reshape(32, 128)
    cap = list_capacity.reshape(16, 128)
    feat = items.T
    lists, own = prep(centroids, feat)
    *kern, item, parts = gen(lists, gather(feat, own))

    for step in range(ITERS - 1):
        parts = lax.all_to_all(parts, "list", 0, 0)
        cols = lax.all_to_all(col_pass(kern, parts, weight), "item", 0, 0)
        parts = row_pass(kern, cols, cap)
    parts = lax.all_to_all(parts, "list", 0, 0)

    early, scale = go((2, 1), True, kern, item, parts, weight)
    came_early = swap_core(early)
    late = go((3, 0), False, kern, item, scale, early)
    came_late = swap_core(late)
    held = (kern, item, scale)
    two = stay(2, 0, BF16, *held, came_early, late)
    one = stay(1, QROWS, BF16, *held, came_early, two)
    three = stay(3, 0, BF16, *held, came_late, one)
    mine = stay(0, QROWS, F32, *held, came_late, three)
    done = finish(mine, [shift_z(block, d) for block, d in ((two, 2), (one, 1), (three, 3))], lists)

    two, one, three = (shift_z(done, d) for d in (2, 1, 3))
    out = lay(((0, 0), (2, 0), (1, 0), (0, 1), (2, 1)), (done, two, one, swap_core(done), swap_core(two)))
    return lay(((3, 0), (1, 1), (3, 1)), (three, swap_core(one), swap_core(three)), out)


def solution(mesh):
    placed = (P("item", "list"), P("item"), P("list"), P("list", None))
    return jax.shard_map(
        local, mesh=mesh, in_specs=placed, out_specs=P("list", None), check_vma=False
    )
```

```python
import functools
import math

import jax
import jax.numpy as jnp
from jax import lax
from jax.experimental import pallas as pl
from jax.experimental.pallas import tpu as pltpu
from jax.sharding import PartitionSpec as P

E = 256
ITERS = 3
EPS = 1e-06
SHARP = 2.5 * math.sqrt(E) * math.log2(math.e)

ITEM_DEV = 4096
LIST_DEV = 2048
HALF = ITEM_DEV // 2
QUART = ITEM_DEV // 4
N_ITEM = 8
N_LIST = 16

F32 = jnp.float32
BF16 = jnp.bfloat16
VMEM = pltpu.VMEM


def whole(n):
    return [pl.BlockSpec(memory_space=VMEM)] * n


def call(body, args, out, scratch, name, flops=0, limit=4):
    return pl.pallas_call(
        body,
        out_shape=out,
        in_specs=whole(len(args)),
        out_specs=tuple(whole(len(out))) if isinstance(out, tuple) else whole(1)[0],
        scratch_shapes=scratch,
        compiler_params=pltpu.CompilerParams(vmem_limit_bytes=limit << 20),
        cost_estimate=pl.CostEstimate(flops=flops, bytes_accessed=1 << 20, transcendentals=0),
        name=name,
    )(*args)


def unit(values, axis):
    square = jnp.mean(values * values, axis=axis, keepdims=True)
    return values * lax.rsqrt(square + EPS) * E ** (-0.5)


def place():
    item = lax.axis_index("item")
    spot = lax.axis_index("list")
    return item % 2, item // 2, spot // 4, spot % 4


def swap_core(block):
    return lax.ppermute(block, "item", [(i, i ^ 1) for i in range(N_ITEM)])


def shift_plane(block, first, step):
    pairs = []
    for i in range(N_ITEM):
        for spot in range(N_LIST):
            if (i % 2 == 0) == first:
                to = spot // 4 * 4 + (spot + step) % 4
            else:
                to = (spot + 4 * step) % N_LIST
            pairs.append((i * N_LIST + spot, i * N_LIST + to))
    return lax.ppermute(block, ("item", "list"), pairs)


ORDER = (0, -1, 1, 2)


def gather(feat, own):
    came = [own] + [shift_plane(feat, True, d) for d in (1, 3, 2)]
    one, two = (jnp.concatenate([c[:, HALF * h : HALF * (h + 1)] for c in came], 0) for h in range(2))
    left_one, right_two = shift_plane(one, False, 1), shift_plane(two, False, 3)
    left_two, right_one = shift_plane(two, False, 1), shift_plane(one, False, 3)
    far_one, far_two = shift_plane(left_one, False, 1), shift_plane(right_two, False, 3)
    return [one, left_one, right_one, far_one, two, left_two, right_two, far_two]


def prep_body(cent_ref, feat_ref, list_ref, own_ref, raw_ref, sems):
    parts = [pl.ds(512 * m, 512) for m in range(4)]
    copies = [pltpu.make_async_copy(cent_ref.at[p, :], raw_ref.at[p, :], sems.at[m]) for m, p in enumerate(parts)]
    copies.append(pltpu.make_async_copy(feat_ref, own_ref, sems.at[4]))
    for copy in copies:
        copy.start()
    for copy, p in zip(copies, parts):
        copy.wait()
        list_ref[p, :] = unit(raw_ref[p, :].astype(F32), 1).astype(BF16)
    copies[4].wait()


def prep(cent, feat):
    return pl.pallas_call(
        prep_body,
        out_shape=(VMEM((LIST_DEV, E), BF16), VMEM(feat.shape, BF16)),
        in_specs=[pl.BlockSpec(memory_space=pltpu.HBM)] * 2,
        out_specs=tuple(whole(2)),
        scratch_shapes=[VMEM((LIST_DEV, E), BF16), pltpu.SemaphoreType.DMA((5,))],
        compiler_params=pltpu.CompilerParams(vmem_limit_bytes=4 << 20),
        cost_estimate=pl.CostEstimate(flops=1 << 20, bytes_accessed=1 << 21, transcendentals=0),
        name="lists",
    )(cent, feat)


def put_rows(total, out_ref):
    rows = jnp.concatenate([total[:, 128 * k : 128 * (k + 1)] for k in range(32)], 0)
    out_ref[...] = jnp.broadcast_to(rows.astype(BF16)[None], (N_LIST, 32, 128))


TILE_M = 256


def gen_body(list_ref, *refs):
    piece_refs, (*kern_refs, item_ref, rows_ref, feat_ref) = refs[:8], refs[8:]
    core, _, y, x = place()
    for i, ref in enumerate(piece_refs):
        outer, at = ORDER[i % 4], slice(HALF * (i // 4), HALF * (i // 4 + 1))
        for j, inner in enumerate(ORDER):
            from_y = (y + jnp.where(core == 0, outer, inner) + 4) % 4
            from_x = (x + jnp.where(core == 0, inner, outer) + 4) % 4
            spot = from_y * 4 + from_x
            feat_ref[pl.ds(pl.multiple_of(spot * 16, 16), 16), at] = ref[16 * j : 16 * (j + 1), :]

    totals = []
    for n, kern_ref in enumerate(kern_refs):
        at = slice(QUART * n, QUART * (n + 1))
        block = feat_ref[:, at]
        wide = block.astype(F32)
        norm = lax.rsqrt(jnp.mean(wide * wide, axis=0, keepdims=True) + EPS) * E ** (-0.5)
        item_ref[at, :] = (wide * norm).T.astype(BF16)
        norm = norm * SHARP
        total = jnp.zeros((8, QUART), F32)
        for m in range(LIST_DEV // TILE_M):
            rows = slice(TILE_M * m, TILE_M * (m + 1))
            score = jnp.dot(list_ref[rows, :], block, preferred_element_type=F32)
            value = jnp.exp2(score * norm)
            kern_ref[rows, :] = value
            total = total + value.reshape(TILE_M // 8, 8, QUART).sum(0)
        totals.append(total.sum(0, keepdims=True))
    put_rows(jnp.concatenate(totals, 1), rows_ref)


def gen(lists, pieces):
    out = (VMEM((LIST_DEV, QUART), F32),) * 4 + (VMEM((ITEM_DEV, E), BF16), VMEM((N_LIST, 32, 128), BF16))
    return call(gen_body, (lists, *pieces), out, [VMEM((E, ITEM_DEV), BF16)], "generate", 2 * LIST_DEV * ITEM_DEV * E, 8)


def spread_rows(parts_ref, weight_ref, scale_ref):
    scale = weight_ref[...] / parts_ref[...].astype(F32).sum(0)
    for k in range(32):
        scale_ref[:, 128 * k : 128 * (k + 1)] = jnp.broadcast_to(scale[k : k + 1, :], (8, 128))


def lane(partial):
    return partial.T.sum(0, keepdims=True)


def col_body(*refs):
    *kern_refs, parts_ref, weight_ref, out_ref, scale_ref = refs
    spread_rows(parts_ref, weight_ref, scale_ref)
    cols = []
    for m in range(LIST_DEV // 128):
        at = slice(128 * m, 128 * (m + 1))
        total = jnp.zeros((16, 8, 128), F32)
        for h, ref in enumerate(kern_refs):
            for n in range(QUART // 128):
                by = scale_ref[:, QUART * h + 128 * n : QUART * h + 128 * (n + 1)]
                total = total + ref[at, 128 * n : 128 * (n + 1)].reshape(16, 8, 128) * by[None]
        cols.append(lane(total.reshape(128, 128)))
    out_ref[...] = jnp.broadcast_to(jnp.concatenate(cols, 0)[None], (N_ITEM, 16, 128))


def col_pass(kern, parts, weight):
    return call(
        col_body, (*kern, parts, weight), VMEM((N_ITEM, 16, 128), F32), [VMEM((8, ITEM_DEV), F32)],
        "columns", 2 * LIST_DEV * ITEM_DEV,
    )


def row_body(*refs):
    *kern_refs, cols_ref, cap_ref, out_ref, scale_ref, total_ref = refs
    scale = cap_ref[...] / cols_ref[...].sum(0)
    for k in range(16):
        scale_ref[128 * k : 128 * (k + 1), :] = jnp.broadcast_to(scale[k : k + 1, :], (128, 128)).T

    for h in range(0, 4, 2):

        def step(m, total):
            at = pl.ds(pl.multiple_of(m * 128, 128), 128)
            by = scale_ref[at, :].reshape(16, 8, 128)
            blocks = [ref[at, :].reshape(16, 8, QUART) for ref in kern_refs[h : h + 2]]
            total = list(total)
            for j in range(16):
                for k in range(16):
                    lanes = slice(128 * (k % 8), 128 * (k % 8 + 1))
                    total[k] = total[k] + blocks[k // 8][j, :, lanes] * by[j]
            return tuple(total)

        total = lax.fori_loop(0, LIST_DEV // 128, step, (jnp.zeros((8, 128), F32),) * 16)
        for k in range(16):
            first = QUART * h + 128 * k
            total_ref[:, first : first + 128] = total[k].sum(0, keepdims=True)

    put_rows(total_ref[...], out_ref)


def row_pass(kern, cols, cap):
    return call(
        row_body, (*kern, cols, cap), VMEM((N_LIST, 32, 128), BF16),
        [VMEM((LIST_DEV, 128), F32), VMEM((1, ITEM_DEV), F32)], "rows", 2 * LIST_DEV * ITEM_DEV,
    )


QROWS = 272


def pack(mixed, col, dtype):
    high = col.astype(BF16).astype(F32)
    tail = jnp.concatenate([jnp.concatenate([high, col - high], 1), jnp.zeros((14, E), F32)], 0)
    return jnp.concatenate([mixed, tail], 0).astype(dtype)


def unpack(ref, first=0):
    block = ref[first : first + QROWS, :].astype(F32)
    return block[:256], block[256:258, :128] + block[256:258, 128:]


def quarter(kern_refs, item_ref, scale_ref, half, number):
    at = pl.ds(pl.multiple_of(half * 1024 + number * 256, 256), 256)
    total = jnp.zeros((32, 8, 128), F32)
    mixed = jnp.zeros((256, E), F32)
    for h, ref in enumerate(kern_refs):
        for n in range(QUART // 256):
            first = QUART * h + 256 * n
            block = ref[at, 256 * n : 256 * (n + 1)].reshape(32, 8, 256)
            block = block * scale_ref[:, first : first + 256][None]
            total = total + block[:, :, :128] + block[:, :, 128:]
            block = block.reshape(256, 256).astype(BF16)
            mixed = mixed + jnp.dot(block, item_ref[first : first + 256, :], preferred_element_type=F32)
    total = total.reshape(256, 128)
    return mixed, jnp.concatenate([lane(total[:128]), lane(total[128:])], 0)


def go_body(fars, new, *refs):
    if new:
        *kern_refs, item_ref, parts_ref, weight_ref, out_ref, scale_ref = refs
        spread_rows(parts_ref, weight_ref, scale_ref)
    else:
        *kern_refs, item_ref, scale_ref, _, out_ref = refs
    core, z, _, _ = place()
    for i, far in enumerate(fars):
        mixed, col = quarter(kern_refs, item_ref, scale_ref, 1 - core, (z + far) % 4)
        out_ref[QROWS * i : QROWS * (i + 1), :] = pack(mixed, col, BF16)


def go(fars, new, kern, item, *more):
    out = VMEM((QROWS * len(fars), E), BF16)
    if new:
        out = (out, VMEM((8, ITEM_DEV), F32))
    body = functools.partial(go_body, fars, new)
    return call(body, (*kern, item, *more), out, [], "totals", LIST_DEV * ITEM_DEV * E)


def stay_body(far, first, *refs):
    *kern_refs, item_ref, scale_ref, came_ref, _, out_ref = refs
    core, z, _, _ = place()
    mixed, col = quarter(kern_refs, item_ref, scale_ref, core, (z + far) % 4)
    came_mixed, came_col = unpack(came_ref, first)
    out_ref[...] = pack(mixed + came_mixed, col + came_col, out_ref.dtype)


def stay(far, first, dtype, kern, item, scale, came, after):
    body = functools.partial(stay_body, far, first)
    return call(body, (*kern, item, scale, came, after), VMEM((QROWS, E), dtype), [], "stay", LIST_DEV * ITEM_DEV * E)


def finish_body(mine_ref, a_ref, b_ref, c_ref, list_ref, out_ref):
    core, z, _, _ = place()
    first = pl.multiple_of(core * 1024 + z * 256, 256)
    totals, cols = (sum(parts) for parts in zip(*(unpack(ref) for ref in (mine_ref, a_ref, b_ref, c_ref))))
    for t in range(2):
        col = jnp.broadcast_to(cols[t : t + 1], (128, 128)).T
        col = jnp.concatenate([col, col], 1)
        own = list_ref[pl.ds(first + 128 * t, 128), :].astype(F32)
        mixed = 0.1 * own + totals[128 * t : 128 * (t + 1)] / col
        out_ref[128 * t : 128 * (t + 1), :] = unit(mixed, 1).astype(BF16)


def finish(mine, came, lists):
    return call(finish_body, (mine, *came, lists), VMEM((256, E), BF16), [], "finish")


def shift_z(block, step):
    return lax.ppermute(block, "item", [(i, (i + 2 * step) % N_ITEM) for i in range(N_ITEM)])


def lay_body(spots, more, *refs):
    blocks, (out_ref, sems) = refs[more:-2], refs[-2:]
    core, z, _, _ = place()
    copies = []
    for i, ((back, other), ref) in enumerate(zip(spots, blocks)):
        half = 1 - core if other else core
        row = pl.multiple_of(half * 1024 + (z - back + 4) % 4 * 256, 256)
        copies.append(pltpu.make_async_copy(ref, out_ref.at[pl.ds(row, 256), :], sems.at[i]))
    for copy in copies:
        copy.start()
    for copy in copies:
        copy.wait()


def lay(spots, blocks, out=None):
    n = len(spots)
    more = int(out is not None)
    place_any = pl.BlockSpec(memory_space=pl.ANY)
    return pl.pallas_call(
        functools.partial(lay_body, spots, more),
        out_shape=jax.ShapeDtypeStruct((LIST_DEV, E), BF16),
        in_specs=[place_any] * more + whole(n),
        out_specs=place_any,
        input_output_aliases={0: 0} if more else {},
        scratch_shapes=[pltpu.SemaphoreType.DMA((n,))],
        compiler_params=pltpu.CompilerParams(vmem_limit_bytes=4 << 20),
        name="lay",
    )(*([out] if more else []), *blocks)


def local(items, item_weight, list_capacity, centroids):
    weight = item_weight.reshape(32, 128)
    cap = list_capacity.reshape(16, 128)
    feat = items.T
    lists, own = prep(centroids, feat)
    *kern, item, parts = gen(lists, gather(feat, own))

    for step in range(ITERS - 1):
        parts = lax.all_to_all(parts, "list", 0, 0)
        cols = lax.all_to_all(col_pass(kern, parts, weight), "item", 0, 0)
        parts = row_pass(kern, cols, cap)
    parts = lax.all_to_all(parts, "list", 0, 0)

    early, scale = go((2, 1), True, kern, item, parts, weight)
    came_early = swap_core(early)
    late = go((3, 0), False, kern, item, scale, early)
    came_late = swap_core(late)
    held = (kern, item, scale)
    two = stay(2, 0, BF16, *held, came_early, late)
    one = stay(1, QROWS, BF16, *held, came_early, two)
    three = stay(3, 0, BF16, *held, came_late, one)
    mine = stay(0, QROWS, F32, *held, came_late, three)
    done = finish(mine, [shift_z(block, d) for block, d in ((two, 2), (one, 1), (three, 3))], lists)

    two, one, three = (shift_z(done, d) for d in (2, 1, 3))
    out = lay(((0, 0), (2, 0), (1, 0), (0, 1), (2, 1)), (done, two, one, swap_core(done), swap_core(two)))
    return lay(((3, 0), (1, 1), (3, 1)), (three, swap_core(one), swap_core(three)), out)


def solution(mesh):
    placed = (P("item", "list"), P("item"), P("list"), P("list", None))
    return jax.shard_map(
        local, mesh=mesh, in_specs=placed, out_specs=P("list", None), check_vma=False
    )
```

```python
import functools
import math

import jax
import jax.numpy as jnp
from jax import lax
from jax.experimental import pallas as pl
from jax.experimental.pallas import tpu as pltpu
from jax.sharding import PartitionSpec as P

E = 256
ITERS = 3
EPS = 1e-06
SHARP = 2.5 * math.sqrt(E) * math.log2(math.e)

ITEM_DEV = 4096
LIST_DEV = 2048
HALF = ITEM_DEV // 2
QUART = ITEM_DEV // 4
N_ITEM = 8
N_LIST = 16

F32 = jnp.float32
BF16 = jnp.bfloat16
VMEM = pltpu.VMEM


def whole(n):
    return [pl.BlockSpec(memory_space=VMEM)] * n


def call(body, args, out, scratch, name, flops=0, limit=4):
    return pl.pallas_call(
        body,
        out_shape=out,
        in_specs=whole(len(args)),
        out_specs=tuple(whole(len(out))) if isinstance(out, tuple) else whole(1)[0],
        scratch_shapes=scratch,
        compiler_params=pltpu.CompilerParams(vmem_limit_bytes=limit << 20),
        cost_estimate=pl.CostEstimate(flops=flops, bytes_accessed=1 << 20, transcendentals=0),
        name=name,
    )(*args)


def unit(values, axis):
    square = jnp.mean(values * values, axis=axis, keepdims=True)
    return values * lax.rsqrt(square + EPS) * E ** (-0.5)


def place():
    item = lax.axis_index("item")
    spot = lax.axis_index("list")
    return item % 2, item // 2, spot // 4, spot % 4


def swap_core(block):
    return lax.ppermute(block, "item", [(i, i ^ 1) for i in range(N_ITEM)])


def shift_plane(block, first, step):
    pairs = []
    for i in range(N_ITEM):
        for spot in range(N_LIST):
            if (i % 2 == 0) == first:
                to = spot // 4 * 4 + (spot + step) % 4
            else:
                to = (spot + 4 * step) % N_LIST
            pairs.append((i * N_LIST + spot, i * N_LIST + to))
    return lax.ppermute(block, ("item", "list"), pairs)


ORDER = (0, -1, 1, 2)


def gather(feat, own):
    came = [own] + [shift_plane(feat, True, d) for d in (1, 3, 2)]
    one, two = (jnp.concatenate([c[:, HALF * h : HALF * (h + 1)] for c in came], 0) for h in range(2))
    left_one, right_two = shift_plane(one, False, 1), shift_plane(two, False, 3)
    left_two, right_one = shift_plane(two, False, 1), shift_plane(one, False, 3)
    far_one, far_two = shift_plane(left_one, False, 1), shift_plane(right_two, False, 3)
    return [one, left_one, right_one, far_one, two, left_two, right_two, far_two]


def prep_body(cent_ref, feat_ref, list_ref, own_ref, raw_ref, sems):
    parts = [pl.ds(512 * m, 512) for m in range(4)]
    copies = [pltpu.make_async_copy(cent_ref.at[p, :], raw_ref.at[p, :], sems.at[m]) for m, p in enumerate(parts)]
    copies.append(pltpu.make_async_copy(feat_ref, own_ref, sems.at[4]))
    for copy in copies:
        copy.start()
    for copy, p in zip(copies, parts):
        copy.wait()
        list_ref[p, :] = unit(raw_ref[p, :].astype(F32), 1).astype(BF16)
    copies[4].wait()


def prep(cent, feat):
    return pl.pallas_call(
        prep_body,
        out_shape=(VMEM((LIST_DEV, E), BF16), VMEM(feat.shape, BF16)),
        in_specs=[pl.BlockSpec(memory_space=pltpu.HBM)] * 2,
        out_specs=tuple(whole(2)),
        scratch_shapes=[VMEM((LIST_DEV, E), BF16), pltpu.SemaphoreType.DMA((5,))],
        compiler_params=pltpu.CompilerParams(vmem_limit_bytes=4 << 20),
        cost_estimate=pl.CostEstimate(flops=1 << 20, bytes_accessed=1 << 21, transcendentals=0),
        name="lists",
    )(cent, feat)


def put_rows(total, out_ref):
    rows = jnp.concatenate([total[:, 128 * k : 128 * (k + 1)] for k in range(32)], 0)
    out_ref[...] = jnp.broadcast_to(rows.astype(BF16)[None], (N_LIST, 32, 128))


TILE_M = 256


def gen_body(list_ref, *refs):
    piece_refs, (*kern_refs, item_ref, rows_ref, feat_ref) = refs[:8], refs[8:]
    core, _, y, x = place()
    for i, ref in enumerate(piece_refs):
        outer, at = ORDER[i % 4], slice(HALF * (i // 4), HALF * (i // 4 + 1))
        for j, inner in enumerate(ORDER):
            from_y = (y + jnp.where(core == 0, outer, inner) + 4) % 4
            from_x = (x + jnp.where(core == 0, inner, outer) + 4) % 4
            spot = from_y * 4 + from_x
            feat_ref[pl.ds(pl.multiple_of(spot * 16, 16), 16), at] = ref[16 * j : 16 * (j + 1), :]

    totals = []
    for n, kern_ref in enumerate(kern_refs):
        at = slice(QUART * n, QUART * (n + 1))
        block = feat_ref[:, at]
        wide = block.astype(F32)
        norm = lax.rsqrt(jnp.mean(wide * wide, axis=0, keepdims=True) + EPS) * E ** (-0.5)
        item_ref[at, :] = (wide * norm).T.astype(BF16)
        norm = norm * SHARP
        total = jnp.zeros((8, QUART), F32)
        for m in range(LIST_DEV // TILE_M):
            rows = slice(TILE_M * m, TILE_M * (m + 1))
            score = jnp.dot(list_ref[rows, :], block, preferred_element_type=F32)
            value = jnp.exp2(score * norm)
            kern_ref[rows, :] = value
            total = total + value.reshape(TILE_M // 8, 8, QUART).sum(0)
        totals.append(total.sum(0, keepdims=True))
    put_rows(jnp.concatenate(totals, 1), rows_ref)


def gen(lists, pieces):
    out = (VMEM((LIST_DEV, QUART), F32),) * 4 + (VMEM((ITEM_DEV, E), BF16), VMEM((N_LIST, 32, 128), BF16))
    return call(gen_body, (lists, *pieces), out, [VMEM((E, ITEM_DEV), BF16)], "generate", 2 * LIST_DEV * ITEM_DEV * E, 8)


def spread_rows(parts_ref, weight_ref, scale_ref):
    scale = weight_ref[...] / parts_ref[...].astype(F32).sum(0)
    for k in range(32):
        scale_ref[:, 128 * k : 128 * (k + 1)] = jnp.broadcast_to(scale[k : k + 1, :], (8, 128))


def lane(partial):
    return partial.T.sum(0, keepdims=True)


def col_body(*refs):
    *kern_refs, parts_ref, weight_ref, out_ref, scale_ref = refs
    spread_rows(parts_ref, weight_ref, scale_ref)
    cols = []
    for m in range(LIST_DEV // 128):
        at = slice(128 * m, 128 * (m + 1))
        total = jnp.zeros((16, 8, 128), F32)
        for h, ref in enumerate(kern_refs):
            for n in range(QUART // 128):
                by = scale_ref[:, QUART * h + 128 * n : QUART * h + 128 * (n + 1)]
                total = total + ref[at, 128 * n : 128 * (n + 1)].reshape(16, 8, 128) * by[None]
        cols.append(lane(total.reshape(128, 128)))
    out_ref[...] = jnp.broadcast_to(jnp.concatenate(cols, 0)[None], (N_ITEM, 16, 128))


def col_pass(kern, parts, weight):
    return call(
        col_body, (*kern, parts, weight), VMEM((N_ITEM, 16, 128), F32), [VMEM((8, ITEM_DEV), F32)],
        "columns", 2 * LIST_DEV * ITEM_DEV,
    )


def row_body(*refs):
    *kern_refs, cols_ref, cap_ref, out_ref, scale_ref, total_ref = refs
    scale = cap_ref[...] / cols_ref[...].sum(0)
    for k in range(16):
        scale_ref[128 * k : 128 * (k + 1), :] = jnp.broadcast_to(scale[k : k + 1, :], (128, 128)).T

    for h in range(0, 4, 2):

        def step(m, total):
            at = pl.ds(pl.multiple_of(m * 128, 128), 128)
            by = scale_ref[at, :].reshape(16, 8, 128)
            blocks = [ref[at, :].reshape(16, 8, QUART) for ref in kern_refs[h : h + 2]]
            total = list(total)
            for j in range(16):
                for k in range(16):
                    lanes = slice(128 * (k % 8), 128 * (k % 8 + 1))
                    total[k] = total[k] + blocks[k // 8][j, :, lanes] * by[j]
            return tuple(total)

        total = lax.fori_loop(0, LIST_DEV // 128, step, (jnp.zeros((8, 128), F32),) * 16)
        for k in range(16):
            first = QUART * h + 128 * k
            total_ref[:, first : first + 128] = total[k].sum(0, keepdims=True)

    put_rows(total_ref[...], out_ref)


def row_pass(kern, cols, cap):
    return call(
        row_body, (*kern, cols, cap), VMEM((N_LIST, 32, 128), BF16),
        [VMEM((LIST_DEV, 128), F32), VMEM((1, ITEM_DEV), F32)], "rows", 2 * LIST_DEV * ITEM_DEV,
    )


QROWS = 272


def pack(mixed, col, dtype):
    high = col.astype(BF16).astype(F32)
    tail = jnp.concatenate([jnp.concatenate([high, col - high], 1), jnp.zeros((14, E), F32)], 0)
    return jnp.concatenate([mixed, tail], 0).astype(dtype)


def unpack(ref, first=0):
    block = ref[first : first + QROWS, :].astype(F32)
    return block[:256], block[256:258, :128] + block[256:258, 128:]


def quarter(kern_refs, item_ref, scale_ref, half, number):
    at = pl.ds(pl.multiple_of(half * 1024 + number * 256, 256), 256)
    total = jnp.zeros((32, 8, 128), F32)
    mixed = jnp.zeros((256, E), F32)
    for h, ref in enumerate(kern_refs):
        for n in range(QUART // 256):
            first = QUART * h + 256 * n
            block = ref[at, 256 * n : 256 * (n + 1)].reshape(32, 8, 256)
            block = block * scale_ref[:, first : first + 256][None]
            total = total + block[:, :, :128] + block[:, :, 128:]
            block = block.reshape(256, 256).astype(BF16)
            mixed = mixed + jnp.dot(block, item_ref[first : first + 256, :], preferred_element_type=F32)
    total = total.reshape(256, 128)
    return mixed, jnp.concatenate([lane(total[:128]), lane(total[128:])], 0)


def go_body(fars, new, *refs):
    if new:
        *kern_refs, item_ref, parts_ref, weight_ref, out_ref, scale_ref = refs
        spread_rows(parts_ref, weight_ref, scale_ref)
    else:
        *kern_refs, item_ref, scale_ref, _, out_ref = refs
    core, z, _, _ = place()
    for i, far in enumerate(fars):
        mixed, col = quarter(kern_refs, item_ref, scale_ref, 1 - core, (z + far) % 4)
        out_ref[QROWS * i : QROWS * (i + 1), :] = pack(mixed, col, BF16)


def go(fars, new, kern, item, *more):
    out = VMEM((QROWS * len(fars), E), BF16)
    if new:
        out = (out, VMEM((8, ITEM_DEV), F32))
    body = functools.partial(go_body, fars, new)
    return call(body, (*kern, item, *more), out, [], "totals", LIST_DEV * ITEM_DEV * E)


def stay_body(far, first, *refs):
    *kern_refs, item_ref, scale_ref, came_ref, _, out_ref = refs
    core, z, _, _ = place()
    mixed, col = quarter(kern_refs, item_ref, scale_ref, core, (z + far) % 4)
    came_mixed, came_col = unpack(came_ref, first)
    out_ref[...] = pack(mixed + came_mixed, col + came_col, out_ref.dtype)


def stay(far, first, dtype, kern, item, scale, came, after):
    body = functools.partial(stay_body, far, first)
    return call(body, (*kern, item, scale, came, after), VMEM((QROWS, E), dtype), [], "stay", LIST_DEV * ITEM_DEV * E)


def finish_body(mine_ref, a_ref, b_ref, c_ref, list_ref, out_ref):
    core, z, _, _ = place()
    first = pl.multiple_of(core * 1024 + z * 256, 256)
    totals, cols = (sum(parts) for parts in zip(*(unpack(ref) for ref in (mine_ref, a_ref, b_ref, c_ref))))
    for t in range(2):
        col = jnp.broadcast_to(cols[t : t + 1], (128, 128)).T
        col = jnp.concatenate([col, col], 1)
        own = list_ref[pl.ds(first + 128 * t, 128), :].astype(F32)
        mixed = 0.1 * own + totals[128 * t : 128 * (t + 1)] / col
        out_ref[128 * t : 128 * (t + 1), :] = unit(mixed, 1).astype(BF16)


def finish(mine, came, lists):
    return call(finish_body, (mine, *came, lists), VMEM((256, E), BF16), [], "finish")


def shift_z(block, step):
    return lax.ppermute(block, "item", [(i, (i + 2 * step) % N_ITEM) for i in range(N_ITEM)])


def lay_body(spots, more, *refs):
    blocks, (out_ref, sems) = refs[more:-2], refs[-2:]
    core, z, _, _ = place()
    copies = []
    for i, ((back, other), ref) in enumerate(zip(spots, blocks)):
        half = 1 - core if other else core
        row = pl.multiple_of(half * 1024 + (z - back + 4) % 4 * 256, 256)
        copies.append(pltpu.make_async_copy(ref, out_ref.at[pl.ds(row, 256), :], sems.at[i]))
    for copy in copies:
        copy.start()
    for copy in copies:
        copy.wait()


def lay(spots, blocks, out=None):
    n = len(spots)
    more = int(out is not None)
    place_any = pl.BlockSpec(memory_space=pl.ANY)
    return pl.pallas_call(
        functools.partial(lay_body, spots, more),
        out_shape=jax.ShapeDtypeStruct((LIST_DEV, E), BF16),
        in_specs=[place_any] * more + whole(n),
        out_specs=place_any,
        input_output_aliases={0: 0} if more else {},
        scratch_shapes=[pltpu.SemaphoreType.DMA((n,))],
        compiler_params=pltpu.CompilerParams(vmem_limit_bytes=4 << 20),
        name="lay",
    )(*([out] if more else []), *blocks)


def local(items, item_weight, list_capacity, centroids):
    weight = item_weight.reshape(32, 128)
    cap = list_capacity.reshape(16, 128)
    feat = items.T
    lists, own = prep(centroids, feat)
    *kern, item, parts = gen(lists, gather(feat, own))

    for step in range(ITERS - 1):
        parts = lax.all_to_all(parts, "list", 0, 0)
        cols = lax.all_to_all(col_pass(kern, parts, weight), "item", 0, 0)
        parts = row_pass(kern, cols, cap)
    parts = lax.all_to_all(parts, "list", 0, 0)

    early, scale = go((2, 1), True, kern, item, parts, weight)
    came_early = swap_core(early)
    late = go((3, 0), False, kern, item, scale, early)
    came_late = swap_core(late)
    held = (kern, item, scale)
    two = stay(2, 0, BF16, *held, came_early, late)
    one = stay(1, QROWS, BF16, *held, came_early, two)
    three = stay(3, 0, BF16, *held, came_late, one)
    mine = stay(0, QROWS, F32, *held, came_late, three)
    done = finish(mine, [shift_z(block, d) for block, d in ((two, 2), (one, 1), (three, 3))], lists)

    three, one, two = (shift_z(done, d) for d in (3, 1, 2))
    out = lay(((0, 0), (2, 0), (1, 0), (3, 0), (0, 1), (2, 1)), (done, two, one, three, swap_core(done), swap_core(two)))
    return lay(((1, 1), (3, 1)), (swap_core(one), swap_core(three)), out)


def solution(mesh):
    placed = (P("item", "list"), P("item"), P("list"), P("list", None))
    return jax.shard_map(
        local, mesh=mesh, in_specs=placed, out_specs=P("list", None), check_vma=False
    )
```

```python
import functools
import math

import jax
import jax.numpy as jnp
from jax import lax
from jax.experimental import pallas as pl
from jax.experimental.pallas import tpu as pltpu
from jax.sharding import PartitionSpec as P

E = 256
ITERS = 3
EPS = 1e-06
SHARP = 2.5 * math.sqrt(E) * math.log2(math.e)

ITEM_DEV = 4096
LIST_DEV = 2048
HALF = ITEM_DEV // 2
QUART = ITEM_DEV // 4
N_ITEM = 8
N_LIST = 16

F32 = jnp.float32
BF16 = jnp.bfloat16
VMEM = pltpu.VMEM


def whole(n):
    return [pl.BlockSpec(memory_space=VMEM)] * n


def call(body, args, out, scratch, name, flops=0, limit=4):
    return pl.pallas_call(
        body,
        out_shape=out,
        in_specs=whole(len(args)),
        out_specs=tuple(whole(len(out))) if isinstance(out, tuple) else whole(1)[0],
        scratch_shapes=scratch,
        compiler_params=pltpu.CompilerParams(vmem_limit_bytes=limit << 20),
        cost_estimate=pl.CostEstimate(flops=flops, bytes_accessed=1 << 20, transcendentals=0),
        name=name,
    )(*args)


def unit(values, axis):
    square = jnp.mean(values * values, axis=axis, keepdims=True)
    return values * lax.rsqrt(square + EPS) * E ** (-0.5)


def place():
    item = lax.axis_index("item")
    spot = lax.axis_index("list")
    return item % 2, item // 2, spot // 4, spot % 4


def swap_core(block):
    return lax.ppermute(block, "item", [(i, i ^ 1) for i in range(N_ITEM)])


def shift_plane(block, first, step):
    pairs = []
    for i in range(N_ITEM):
        for spot in range(N_LIST):
            if (i % 2 == 0) == first:
                to = spot // 4 * 4 + (spot + step) % 4
            else:
                to = (spot + 4 * step) % N_LIST
            pairs.append((i * N_LIST + spot, i * N_LIST + to))
    return lax.ppermute(block, ("item", "list"), pairs)


ORDER = (0, -1, 1, 2)


def gather(feat, own):
    came = [own] + [shift_plane(feat, True, d) for d in (1, 3, 2)]
    one, two = (jnp.concatenate([c[:, HALF * h : HALF * (h + 1)] for c in came], 0) for h in range(2))
    left_one, right_two = shift_plane(one, False, 1), shift_plane(two, False, 3)
    left_two, right_one = shift_plane(two, False, 1), shift_plane(one, False, 3)
    far_one, far_two = shift_plane(left_one, False, 1), shift_plane(right_two, False, 3)
    return [one, left_one, right_one, far_one, two, left_two, right_two, far_two]


def prep_body(cent_ref, feat_ref, list_ref, own_ref, raw_ref, sems):
    parts = [pl.ds(512 * m, 512) for m in range(4)]
    copies = [pltpu.make_async_copy(cent_ref.at[p, :], raw_ref.at[p, :], sems.at[m]) for m, p in enumerate(parts)]
    copies.append(pltpu.make_async_copy(feat_ref, own_ref, sems.at[4]))
    for copy in copies:
        copy.start()
    for copy, p in zip(copies, parts):
        copy.wait()
        list_ref[p, :] = unit(raw_ref[p, :].astype(F32), 1).astype(BF16)
    copies[4].wait()


def prep(cent, feat):
    return pl.pallas_call(
        prep_body,
        out_shape=(VMEM((LIST_DEV, E), BF16), VMEM(feat.shape, BF16)),
        in_specs=[pl.BlockSpec(memory_space=pltpu.HBM)] * 2,
        out_specs=tuple(whole(2)),
        scratch_shapes=[VMEM((LIST_DEV, E), BF16), pltpu.SemaphoreType.DMA((5,))],
        compiler_params=pltpu.CompilerParams(vmem_limit_bytes=4 << 20),
        cost_estimate=pl.CostEstimate(flops=1 << 20, bytes_accessed=1 << 21, transcendentals=0),
        name="lists",
    )(cent, feat)


def put_rows(total, out_ref):
    rows = jnp.concatenate([total[:, 128 * k : 128 * (k + 1)] for k in range(32)], 0)
    out_ref[...] = jnp.broadcast_to(rows.astype(BF16)[None], (N_LIST, 32, 128))


TILE_M = 256


def gen_body(list_ref, *refs):
    piece_refs, (*kern_refs, item_ref, rows_ref, feat_ref) = refs[:8], refs[8:]
    core, _, y, x = place()
    for i, ref in enumerate(piece_refs):
        outer, at = ORDER[i % 4], slice(HALF * (i // 4), HALF * (i // 4 + 1))
        for j, inner in enumerate(ORDER):
            from_y = (y + jnp.where(core == 0, outer, inner) + 4) % 4
            from_x = (x + jnp.where(core == 0, inner, outer) + 4) % 4
            spot = from_y * 4 + from_x
            feat_ref[pl.ds(pl.multiple_of(spot * 16, 16), 16), at] = ref[16 * j : 16 * (j + 1), :]

    totals = []
    for n, kern_ref in enumerate(kern_refs):
        at = slice(QUART * n, QUART * (n + 1))
        block = feat_ref[:, at]
        wide = block.astype(F32)
        norm = lax.rsqrt(jnp.mean(wide * wide, axis=0, keepdims=True) + EPS) * E ** (-0.5)
        item_ref[at, :] = (wide * norm).T.astype(BF16)
        norm = norm * SHARP
        total = jnp.zeros((8, QUART), F32)
        for m in range(LIST_DEV // TILE_M):
            rows = slice(TILE_M * m, TILE_M * (m + 1))
            score = jnp.dot(list_ref[rows, :], block, preferred_element_type=F32)
            value = jnp.exp2(score * norm)
            kern_ref[rows, :] = value
            total = total + value.reshape(TILE_M // 8, 8, QUART).sum(0)
        totals.append(total.sum(0, keepdims=True))
    put_rows(jnp.concatenate(totals, 1), rows_ref)


def gen(lists, pieces):
    out = (VMEM((LIST_DEV, QUART), F32),) * 4 + (VMEM((ITEM_DEV, E), BF16), VMEM((N_LIST, 32, 128), BF16))
    return call(gen_body, (lists, *pieces), out, [VMEM((E, ITEM_DEV), BF16)], "generate", 2 * LIST_DEV * ITEM_DEV * E, 8)


def spread_rows(parts_ref, weight_ref, scale_ref):
    scale = weight_ref[...] / parts_ref[...].astype(F32).sum(0)
    for k in range(32):
        scale_ref[:, 128 * k : 128 * (k + 1)] = jnp.broadcast_to(scale[k : k + 1, :], (8, 128))


def lane(partial):
    return partial.T.sum(0, keepdims=True)


def col_body(*refs):
    *kern_refs, parts_ref, weight_ref, out_ref, scale_ref = refs
    spread_rows(parts_ref, weight_ref, scale_ref)
    cols = []
    for m in range(LIST_DEV // 128):
        at = slice(128 * m, 128 * (m + 1))
        total = jnp.zeros((16, 8, 128), F32)
        for h, ref in enumerate(kern_refs):
            for n in range(QUART // 128):
                by = scale_ref[:, QUART * h + 128 * n : QUART * h + 128 * (n + 1)]
                total = total + ref[at, 128 * n : 128 * (n + 1)].reshape(16, 8, 128) * by[None]
        cols.append(lane(total.reshape(128, 128)))
    out_ref[...] = jnp.broadcast_to(jnp.concatenate(cols, 0).astype(BF16)[None], (N_ITEM, 16, 128))


def col_pass(kern, parts, weight):
    return call(
        col_body, (*kern, parts, weight), VMEM((N_ITEM, 16, 128), BF16), [VMEM((8, ITEM_DEV), F32)],
        "columns", 2 * LIST_DEV * ITEM_DEV,
    )


def row_body(*refs):
    *kern_refs, cols_ref, cap_ref, out_ref, scale_ref, total_ref = refs
    scale = cap_ref[...] / cols_ref[...].astype(F32).sum(0)
    for k in range(16):
        scale_ref[128 * k : 128 * (k + 1), :] = jnp.broadcast_to(scale[k : k + 1, :], (128, 128)).T

    for h in range(0, 4, 2):

        def step(m, total):
            at = pl.ds(pl.multiple_of(m * 128, 128), 128)
            by = scale_ref[at, :].reshape(16, 8, 128)
            blocks = [ref[at, :].reshape(16, 8, QUART) for ref in kern_refs[h : h + 2]]
            total = list(total)
            for j in range(16):
                for k in range(16):
                    lanes = slice(128 * (k % 8), 128 * (k % 8 + 1))
                    total[k] = total[k] + blocks[k // 8][j, :, lanes] * by[j]
            return tuple(total)

        total = lax.fori_loop(0, LIST_DEV // 128, step, (jnp.zeros((8, 128), F32),) * 16)
        for k in range(16):
            first = QUART * h + 128 * k
            total_ref[:, first : first + 128] = total[k].sum(0, keepdims=True)

    put_rows(total_ref[...], out_ref)


def row_pass(kern, cols, cap):
    return call(
        row_body, (*kern, cols, cap), VMEM((N_LIST, 32, 128), BF16),
        [VMEM((LIST_DEV, 128), F32), VMEM((1, ITEM_DEV), F32)], "rows", 2 * LIST_DEV * ITEM_DEV,
    )


QROWS = 272


def pack(mixed, col, dtype):
    high = col.astype(BF16).astype(F32)
    tail = jnp.concatenate([jnp.concatenate([high, col - high], 1), jnp.zeros((14, E), F32)], 0)
    return jnp.concatenate([mixed, tail], 0).astype(dtype)


def unpack(ref, first=0):
    block = ref[first : first + QROWS, :].astype(F32)
    return block[:256], block[256:258, :128] + block[256:258, 128:]


def quarter(kern_refs, item_ref, scale_ref, half, number):
    at = pl.ds(pl.multiple_of(half * 1024 + number * 256, 256), 256)
    total = jnp.zeros((32, 8, 128), F32)
    mixed = jnp.zeros((256, E), F32)
    for h, ref in enumerate(kern_refs):
        for n in range(QUART // 256):
            first = QUART * h + 256 * n
            block = ref[at, 256 * n : 256 * (n + 1)].reshape(32, 8, 256)
            block = block * scale_ref[:, first : first + 256][None]
            total = total + block[:, :, :128] + block[:, :, 128:]
            block = block.reshape(256, 256).astype(BF16)
            mixed = mixed + jnp.dot(block, item_ref[first : first + 256, :], preferred_element_type=F32)
    total = total.reshape(256, 128)
    return mixed, jnp.concatenate([lane(total[:128]), lane(total[128:])], 0)


def go_body(fars, new, *refs):
    if new:
        *kern_refs, item_ref, parts_ref, weight_ref, out_ref, scale_ref = refs
        spread_rows(parts_ref, weight_ref, scale_ref)
    else:
        *kern_refs, item_ref, scale_ref, _, out_ref = refs
    core, z, _, _ = place()
    for i, far in enumerate(fars):
        mixed, col = quarter(kern_refs, item_ref, scale_ref, 1 - core, (z + far) % 4)
        out_ref[QROWS * i : QROWS * (i + 1), :] = pack(mixed, col, BF16)


def go(fars, new, kern, item, *more):
    out = VMEM((QROWS * len(fars), E), BF16)
    if new:
        out = (out, VMEM((8, ITEM_DEV), F32))
    body = functools.partial(go_body, fars, new)
    return call(body, (*kern, item, *more), out, [], "totals", LIST_DEV * ITEM_DEV * E)


def stay_body(far, first, *refs):
    *kern_refs, item_ref, scale_ref, came_ref, _, out_ref = refs
    core, z, _, _ = place()
    mixed, col = quarter(kern_refs, item_ref, scale_ref, core, (z + far) % 4)
    came_mixed, came_col = unpack(came_ref, first)
    out_ref[...] = pack(mixed + came_mixed, col + came_col, out_ref.dtype)


def stay(far, first, dtype, kern, item, scale, came, after):
    body = functools.partial(stay_body, far, first)
    return call(body, (*kern, item, scale, came, after), VMEM((QROWS, E), dtype), [], "stay", LIST_DEV * ITEM_DEV * E)


def finish_body(mine_ref, a_ref, b_ref, c_ref, list_ref, out_ref):
    core, z, _, _ = place()
    first = pl.multiple_of(core * 1024 + z * 256, 256)
    totals, cols = (sum(parts) for parts in zip(*(unpack(ref) for ref in (mine_ref, a_ref, b_ref, c_ref))))
    for t in range(2):
        col = jnp.broadcast_to(cols[t : t + 1], (128, 128)).T
        col = jnp.concatenate([col, col], 1)
        own = list_ref[pl.ds(first + 128 * t, 128), :].astype(F32)
        mixed = 0.1 * own + totals[128 * t : 128 * (t + 1)] / col
        out_ref[128 * t : 128 * (t + 1), :] = unit(mixed, 1).astype(BF16)


def finish(mine, came, lists):
    return call(finish_body, (mine, *came, lists), VMEM((256, E), BF16), [], "finish")


def shift_z(block, step):
    return lax.ppermute(block, "item", [(i, (i + 2 * step) % N_ITEM) for i in range(N_ITEM)])


def lay_body(spots, more, *refs):
    blocks, (out_ref, sems) = refs[more:-2], refs[-2:]
    core, z, _, _ = place()
    copies = []
    for i, ((back, other), ref) in enumerate(zip(spots, blocks)):
        half = 1 - core if other else core
        row = pl.multiple_of(half * 1024 + (z - back + 4) % 4 * 256, 256)
        copies.append(pltpu.make_async_copy(ref, out_ref.at[pl.ds(row, 256), :], sems.at[i]))
    for copy in copies:
        copy.start()
    for copy in copies:
        copy.wait()


def lay(spots, blocks, out=None):
    n = len(spots)
    more = int(out is not None)
    place_any = pl.BlockSpec(memory_space=pl.ANY)
    return pl.pallas_call(
        functools.partial(lay_body, spots, more),
        out_shape=jax.ShapeDtypeStruct((LIST_DEV, E), BF16),
        in_specs=[place_any] * more + whole(n),
        out_specs=place_any,
        input_output_aliases={0: 0} if more else {},
        scratch_shapes=[pltpu.SemaphoreType.DMA((n,))],
        compiler_params=pltpu.CompilerParams(vmem_limit_bytes=4 << 20),
        name="lay",
    )(*([out] if more else []), *blocks)


def local(items, item_weight, list_capacity, centroids):
    weight = item_weight.reshape(32, 128)
    cap = list_capacity.reshape(16, 128)
    feat = items.T
    lists, own = prep(centroids, feat)
    *kern, item, parts = gen(lists, gather(feat, own))

    for step in range(ITERS - 1):
        parts = lax.all_to_all(parts, "list", 0, 0)
        cols = lax.all_to_all(col_pass(kern, parts, weight), "item", 0, 0)
        parts = row_pass(kern, cols, cap)
    parts = lax.all_to_all(parts, "list", 0, 0)

    early, scale = go((2, 1), True, kern, item, parts, weight)
    came_early = swap_core(early)
    late = go((3, 0), False, kern, item, scale, early)
    came_late = swap_core(late)
    held = (kern, item, scale)
    two = stay(2, 0, BF16, *held, came_early, late)
    one = stay(1, QROWS, BF16, *held, came_early, two)
    three = stay(3, 0, BF16, *held, came_late, one)
    mine = stay(0, QROWS, F32, *held, came_late, three)
    done = finish(mine, [shift_z(block, d) for block, d in ((two, 2), (one, 1), (three, 3))], lists)

    three, one, two = (shift_z(done, d) for d in (3, 1, 2))
    out = lay(((0, 0), (2, 0), (1, 0), (3, 0), (0, 1), (2, 1)), (done, two, one, three, swap_core(done), swap_core(two)))
    return lay(((1, 1), (3, 1)), (swap_core(one), swap_core(three)), out)


def solution(mesh):
    placed = (P("item", "list"), P("item"), P("list"), P("list", None))
    return jax.shard_map(
        local, mesh=mesh, in_specs=placed, out_specs=P("list", None), check_vma=False
    )
```
